32 devices in a mesh: leaf: 8 (over z, x), probe: 4 (over y, core).
Axes of the slice: x: 2, y: 2, z: 4, core: 2. Of those that a mesh axis runs over, the one named last changes fastest.
Arguments:
- covariates: float32 [8, 8192], P(None, 'leaf'), may hold values from -6 to 6
- targets: float32 [8192], P('leaf'), may hold values from -18 to 18
- noise_var: float32 [8192], P('leaf'), may hold values from 0.5 to 2
- lengths: float32 [8], replicated, may hold values from 0.7 to 1.5
- frequencies: float32 [7, 8, 128], replicated, may hold values from -6 to 6
- phases: float32 [7, 128], replicated, may hold values from -3.140625 to 3.140625
- tree_order: int32 [8192], P('leaf'), may hold values from 0 to 8191, each once
- probe_seeds: int32 [64], P('probe'), may hold values from 0 to 16777215
Outputs:
- target_solve: float32 [8192], P('leaf')
- probe_solves: float32 [64, 8192], P('probe', 'leaf')
- noise_grad: float32 [8192], P('leaf')
The draws below stay inside these ranges and needn't reach their ends.
Inputs may be any that keep to these rules, and one draw needn't show every extreme that they name: `tree_order`: each value 0 to 8191 appears exactly once.
All inputs are finite; a program needn't handle non-finite values.
Results may differ from the reference program's by a relative error of at most 0.00021.
Values sent between devices are 32-bit elements; how exact they have to be, the bound alone decides.
No kernel may reach another device: no remote copies, remote signals or barrier semaphores. Data moves between devices by JAX's collectives and lax.ppermute only.
A program may use at most 128 MiB of HBM per device.

```python
import math
import jax
import jax.numpy as jnp
from jax import lax

LEAF = 1024
RANK = 128
COVS = 8
PROBES = 64
N = 8192
NODES = 7
N_LEAF = 8


def with_ends(drawn, stream_key, low, top_value):
    spot = [jax.random.randint(jax.random.fold_in(stream_key, axis), (), 0, length) for axis, length in enumerate(drawn.shape)]
    longest = drawn.shape.index(max(drawn.shape))
    next_to = spot[:longest] + [(spot[longest] + 1) % drawn.shape[longest]] + spot[longest + 1:]
    return drawn.at[tuple(spot)].set(low).at[tuple(next_to)].set(top_value)


def level_of(own_key, extent, shards, smallest, largest):
    def one(position, blocks):
        steps = jax.random.uniform(jax.random.fold_in(jax.random.fold_in(own_key, 6), position), (blocks,), jnp.float32, smallest / len(shards), largest / len(shards))
        return jnp.repeat(jnp.exp(steps), extent[position] // blocks).reshape((-1,) + (1,) * (len(extent) - position - 1))

    level = one(*shards[0])
    for cut in shards[1:]:
        level = level * one(*cut)
    return level


def centred(stream_key, shape, scale, bound, split=(), kind=jnp.bfloat16):
    result = scale * jax.random.normal(stream_key, shape, jnp.float32)
    if split:
        result = result * level_of(stream_key, shape, split, -0.22, 0.18)
    return jnp.clip(result, -bound, bound).astype(kind)


def setup_inputs(seed: int = 0) -> dict:
    key_of = jax.random.split(jax.random.key(seed), 9)
    covariates = centred(key_of[0], (COVS, N), 1.0, 6.0, ((1, 8),), jnp.float32)
    targets = centred(key_of[1], (N,), 3.0, 18.0, ((0, 8),), jnp.float32)
    noise_var = jnp.clip(jnp.exp(math.log(2.0) - 1.3862944 * jax.random.uniform(key_of[2], (N,), jnp.float32) ** level_of(key_of[2], (N,), ((0, 8),), -0.2, 0.2)), 0.5, 2.0)
    lengths = jnp.clip(jnp.exp(jax.random.uniform(key_of[3], (COVS,), jnp.float32, math.log(0.7), math.log(1.5))), 0.7, 1.5)
    frequencies = centred(key_of[4], (NODES, COVS, RANK), 1.0, 6.0, (), jnp.float32)
    phases = jnp.clip(jax.random.uniform(key_of[5], (NODES, RANK), jnp.float32, -3.140625, 3.140625), -3.140625, 3.140625)
    tree_order = jax.random.permutation(key_of[6], N).astype(jnp.int32)
    probe_seeds = with_ends(jax.random.randint(key_of[7], (PROBES,), 0, 16777216), jax.random.fold_in(key_of[7], 1), 0, 16777215).astype(jnp.int32)
    return {"covariates": covariates, "targets": targets, "noise_var": noise_var, "lengths": lengths, "frequencies": frequencies, "phases": phases, "tree_order": tree_order, "probe_seeds": probe_seeds}


highest = lax.Precision.HIGHEST
hash_first = 747796405
hash_second = -1403630843
hash_third = -2073254261

def rademacher(seeds, positions):
    mixed = seeds[:, None] * jnp.int32(hash_first) + positions[None, :] * jnp.int32(hash_second)
    mixed = jnp.bitwise_xor(mixed, lax.shift_right_logical(mixed, jnp.full_like(mixed, 15)))
    mixed = mixed * jnp.int32(hash_third)
    mixed = jnp.bitwise_xor(mixed, lax.shift_right_logical(mixed, jnp.full_like(mixed, 13)))
    parity = jnp.bitwise_and(lax.shift_right_logical(mixed, jnp.full_like(mixed, 11)), jnp.full_like(mixed, 1))
    return (2 * parity - 1).astype(jnp.float32)

def features(coords, omega, phase):
    angle = jnp.dot(omega.T.astype(jnp.float32), coords.astype(jnp.float32), precision=highest, preferred_element_type=jnp.float32) + phase[:, None]
    return jnp.sqrt(2.0 / omega.shape[1]) * jnp.cos(angle)

def leaf_matrix(coords, point_noise, lengths):
    scaled = coords / lengths[:, None]
    squared = lax.optimization_barrier(jnp.sum(scaled * scaled, axis=0))
    cross = jnp.dot(scaled.T.astype(jnp.float32), scaled.astype(jnp.float32), precision=highest, preferred_element_type=jnp.float32)
    return jnp.exp(-0.5 * (squared[:, None] + squared[None, :] - 2.0 * cross)) + jnp.diag(point_noise)

def small_solve(factors, projected):
    return jax.scipy.linalg.cho_solve((factors, True), projected.T)

def reference(covariates, targets, noise_var, lengths, frequencies, phases, tree_order, probe_seeds):
    levels = N_LEAF.bit_length() - 1
    total = LEAF * N_LEAF
    coords = jnp.take(covariates, tree_order, axis=1)
    point_targets = jnp.take(targets, tree_order)
    point_noise = jnp.take(noise_var, tree_order)
    positions = jnp.arange(total, dtype=jnp.int32)
    probe_signs = rademacher(probe_seeds, positions)
    right_sides = jnp.concatenate([point_targets[None, :], probe_signs], axis=0)
    omega_all = frequencies / lengths[None, :, None]

    def leaf_solve(leaf_number):
        start = leaf_number * LEAF
        leaf_coords = lax.dynamic_slice_in_dim(coords, start, LEAF, 1)
        leaf_noise = lax.dynamic_slice_in_dim(point_noise, start, LEAF, 0)
        leaf_rhs = lax.dynamic_slice_in_dim(right_sides, start, LEAF, 1)
        bases = []
        for height in range(1, levels + 1):
            node = jnp.right_shift(N_LEAF + leaf_number, jnp.int32(height))
            bases.append(features(leaf_coords, omega_all[node - 1], phases[node - 1]))
        stacked = jnp.stack(bases)
        factor = jnp.linalg.cholesky(leaf_matrix(leaf_coords, leaf_noise, lengths))
        columns = jnp.concatenate([stacked.reshape(levels * RANK, LEAF), leaf_rhs], axis=0)
        solved_leaf = jax.scipy.linalg.cho_solve((factor, True), columns.T).T
        return (solved_leaf, stacked)
    solved, bases = lax.map(leaf_solve, jnp.arange(N_LEAF, dtype=jnp.int32))
    identity = jnp.eye(RANK, dtype=jnp.float32)
    for height in range(1, levels + 1):
        basis_block = solved[:, :RANK]
        remainder = solved[:, RANK:]
        basis_rows = bases[:, height - 1]
        gram_block = jnp.einsum('jrm,jsm->jrs', basis_block, basis_rows, precision=highest)
        projected = jnp.einsum('jcm,jsm->jcs', remainder, basis_rows, precision=highest)
        groups = N_LEAF >> height
        members = 1 << height
        gram_block = gram_block.reshape(groups, members, RANK, RANK).sum(axis=1)
        projected = projected.reshape(groups, members, remainder.shape[1], RANK).sum(axis=1)
        capacitance = identity + 0.5 * (gram_block + jnp.swapaxes(gram_block, 1, 2))
        factors = jnp.linalg.cholesky(capacitance)
        coefficients = jax.vmap(small_solve)(factors, projected)
        coefficients = jnp.repeat(coefficients, members, axis=0)
        solved = remainder - jnp.einsum('jrc,jrm->jcm', coefficients, basis_block, precision=highest)
    target_solve = solved[:, 0, :].reshape(total)
    probe_solves = jnp.transpose(solved[:, 1:, :], (1, 0, 2)).reshape(PROBES, total)
    estimate = lax.optimization_barrier(jnp.sum(probe_signs * probe_solves, axis=0)) / PROBES
    noise_grad = 0.5 * target_solve * target_solve - 0.5 * estimate
    return (target_solve, probe_solves, noise_grad)
```

```python
import functools
import math

import jax
import jax.numpy as jnp
from jax import lax
from jax.experimental import pallas as pl
from jax.experimental.pallas import tpu as pltpu
from jax.sharding import PartitionSpec as P

PROBES = 64
BLOCK = 256
SETTLED = 1.001

f32 = jnp.float32
bf16 = jnp.bfloat16
highest = lax.Precision.HIGHEST
hash_first = 747796405
hash_second = -1403630843
hash_third = -2073254261
VMEM_BYTES = 40 * 1024 * 1024


def partner_of(block, axis, apart):
    count = lax.axis_size(axis)
    return lax.ppermute(block, axis, [(i, i ^ (1 << apart)) for i in range(count)])


def halves(x):
    high = x.astype(bf16)
    return high, (x - high.astype(f32)).astype(bf16)


def thirds(x):
    high = x.astype(bf16)
    rest = x - high.astype(f32)
    middle = rest.astype(bf16)
    return high, middle, (rest - middle.astype(f32)).astype(bf16)


NN = (((1,), (0,)), ((), ()))
NT = (((1,), (1,)), ((), ()))
TN = (((0,), (0,)), ((), ()))


def dot_one(a, b, dims=NN):
    return lax.dot_general(a, b, dims, preferred_element_type=f32)


def dot_three(a, b, dims=NN):
    a_high, a_low = halves(a)
    b_high, b_low = halves(b)
    return dot_one(a_high, b_high, dims) + (dot_one(a_high, b_low, dims) + dot_one(a_low, b_high, dims))


def dot_full(a, b, dims=NN):
    return lax.dot_general(a, b, dims, precision=highest, preferred_element_type=f32)


def unit(size):
    rows = lax.broadcasted_iota(jnp.int32, (size, size), 0)
    columns = lax.broadcasted_iota(jnp.int32, (size, size), 1)
    return rows == columns


def gain(ratio):
    reach = (ratio - 1.0) / (ratio + 1.0)
    return 2.0 / (2.0 - reach * reach)


def tighter(ratio):
    return (ratio + 1.0) * (ratio + 1.0) / (4.0 * ratio)


def inverse(matrix, low, residual, approx):
    size = matrix.shape[0]
    same = unit(size)
    high = jnp.max(jnp.sum(jnp.abs(matrix), axis=0, keepdims=True)) * 1.0001
    low = jnp.minimum(low, high) * 0.9999
    scale = 2.0 / (low + high)
    ratio = high / low
    c = gain(ratio)
    first = jnp.where(same, 1.0, 0.0) - scale * matrix
    residual[...] = c * dot_three(first, first) - jnp.where(same, c - 1.0, 0.0)
    approx[...] = (c * scale) * (first + jnp.where(same, 1.0, 0.0))

    def more(ratio):
        return tighter(ratio) > SETTLED

    def double(ratio):
        c = gain(ratio)
        e = residual[...]
        x = approx[...]
        squared = dot_three(e, e)
        moved = dot_three(x, e)
        residual[...] = c * squared - jnp.where(same, c - 1.0, 0.0)
        approx[...] = c * (x + moved)
        return tighter(ratio)

    ratio = lax.while_loop(more, double, tighter(ratio))
    x = approx[...]
    x = gain(ratio) * (x + dot_three(x, residual[...]))
    left = jnp.where(same, 1.0, 0.0) - dot_full(x, matrix)
    return x + dot_three(left, x)


def cosine(x):
    turns = jnp.floor(x * (1.0 / math.pi) + 0.5)
    r = x - turns * 3.140625
    r = r - turns * 9.67502593994140625e-4
    r = r - turns * 1.509957990978376e-7
    odd = jnp.bitwise_and(turns.astype(jnp.int32), 1)
    s = r * r
    value = 1.0 / 479001600.0
    for term in (-1.0 / 3628800.0, 1.0 / 40320.0, -1.0 / 720.0, 1.0 / 24.0, -0.5, 1.0):
        value = value * s + term
    return jnp.where(odd == 1, -value, value)


def logical_right(x, by):
    return lax.shift_right_logical(x, jnp.full_like(x, by))


def signs_of(seeds, positions):
    mixed = seeds * jnp.int32(hash_first) + positions * jnp.int32(hash_second)
    mixed = jnp.bitwise_xor(mixed, logical_right(mixed, 15))
    mixed = mixed * jnp.int32(hash_third)
    mixed = jnp.bitwise_xor(mixed, logical_right(mixed, 13))
    parity = jnp.bitwise_and(logical_right(mixed, 11), jnp.full_like(mixed, 1))
    return (2 * parity - 1).astype(f32)


def leaf_kernel(levels, place_ref, data_ref, length_ref, frequency_ref, phase_ref, seed_ref,
                lower_ref, aug_ref, gram_ref, matrix, residual, approx):
    width = data_ref.shape[1]
    rank = frequency_ref.shape[2]
    covs = length_ref.shape[0]
    probes = seed_ref.shape[0]
    blocks = width // BLOCK
    top = width + levels * rank
    u = data_ref[0:covs, :] / length_ref[...]
    s = -0.5 * jnp.sum(u * u, axis=0, keepdims=True)
    u_parts = [p.astype(f32) for p in thirds(u)]
    h, m, l = u_parts
    row = lax.broadcasted_iota(jnp.int32, (8, width), 0)
    ones = jnp.where(row < 3, 1.0, 0.0)
    for level in range(levels):
        node = jnp.right_shift(place_ref[1], level + 1) - 1
        fh, fm, fl = [p.astype(f32) for p in thirds(frequency_ref[node])]
        ph, pm, p_low = [p.astype(f32) for p in thirds(phase_ref[pl.ds(node, 1), :])]
        at_row = lax.broadcasted_iota(jnp.int32, (8, rank), 0)
        phases = jnp.where(at_row == 0, ph, jnp.where(at_row == 1, pm, jnp.where(at_row == 2, p_low, 0.0)))
        left = jnp.concatenate([fh, fh, fm, fm, fh, fl, phases, jnp.zeros_like(phases)], axis=0).astype(bf16)
        right = jnp.concatenate([h, m, h, m, l, h, ones, ones], axis=0).astype(bf16)
        angle = dot_one(left, right, TN)
        matrix[width + level * rank:width + (level + 1) * rank, :] = math.sqrt(2.0 / rank) * cosine(angle)
    positions = place_ref[0] + lax.broadcasted_iota(jnp.int32, (probes, width), 1)
    matrix[top:top + probes, :] = signs_of(seed_ref[...], positions)
    matrix[top + probes:, :] = jnp.concatenate(
        [data_ref[covs:covs + 1, :], jnp.zeros((matrix.shape[0] - top - probes - 1, width), f32)], axis=0)
    s_parts = [p.astype(f32) for p in thirds(s)]
    s_rows = jnp.where(row == 0, s_parts[0], jnp.where(row == 1, s_parts[1], jnp.where(row == 2, s_parts[2], 0.0)))
    left = jnp.concatenate([h, h, m, m, h, l, s_rows, ones], axis=0).astype(bf16)
    right = jnp.concatenate([h, m, h, m, l, h, ones, s_rows], axis=0).astype(bf16)
    noise = data_ref[covs + 1:covs + 2, :]
    same = unit(BLOCK)
    spans = [slice(k * BLOCK, (k + 1) * BLOCK) for k in range(blocks)]
    for i in range(blocks):
        for j in range(i + 1):
            part = jnp.exp(dot_one(left[:, spans[i]], right[:, spans[j]], TN))
            if i == j:
                part = part + jnp.where(same, noise[:, spans[i]], 0.0)
            matrix[spans[i], spans[j]] = part
    rows = matrix.shape[0]
    for k in range(blocks):
        block_inverse = inverse(matrix[spans[k], spans[k]], jnp.min(noise[:, spans[k]]), residual, approx)
        below = (k + 1) * BLOCK
        column = matrix[below:, spans[k]]
        weights = dot_full(column, block_inverse)
        for j in range(k + 1, blocks):
            start = j * BLOCK
            matrix[start:, spans[j]] = matrix[start:, spans[j]] - dot_full(
                weights[start - below:], column[start - below:start - below + BLOCK], NT)
        at = 0
        for level in range(levels):
            start = width + level * rank
            part = dot_full(weights[start - below:], column[start - below:start - below + rank], NT)
            count = rows - start
            if k == 0:
                gram_ref[at:at + count, :] = part
            else:
                gram_ref[at:at + count, :] += part
            at += count
        aug_ref[:, spans[k]] = weights[width - below:]
        if k + 1 < blocks:
            lower_ref[k * BLOCK:, spans[k]] = weights[:width - below]


def eliminate(own, other, rank, residual, approx):
    total = own + other
    capacitance = total[:rank] + jnp.where(unit(rank), 1.0, 0.0)
    return total, dot_full(total[rank:], inverse(capacitance, jnp.float32(1.0), residual, approx))


def height_kernel(left, tail, own_ref, other_ref, coefficient_ref, rest_ref, residual, approx):
    rank = own_ref.shape[1]
    count = left * rank + tail
    total, coefficients = eliminate(own_ref[:count, :], other_ref[:count, :], rank, residual, approx)
    coefficient_ref[...] = coefficients
    at, to = count, 0
    for level in range(1, left):
        size = (left - level) * rank + tail
        start = (level - 1) * rank
        rest_ref[to:to + size, :] = own_ref[at:at + size, :] + other_ref[at:at + size, :] - dot_full(
            coefficients[start:], total[level * rank:(level + 1) * rank], NT)
        at += size
        to += size


def final_kernel(levels, probes, tail, *refs):
    own_ref, other_ref = refs[:2]
    coefficient_refs = refs[2:2 + levels - 1]
    lower_ref, aug_ref, seed_ref, first_ref = refs[1 + levels:5 + levels]
    target_ref, solve_ref, terms_ref, residual, approx = refs[5 + levels:]
    rank = own_ref.shape[1]
    width = aug_ref.shape[1]
    blocks = width // BLOCK
    _, last = eliminate(own_ref[...], other_ref[...], rank, residual, approx)
    combined = [None] * levels
    combined[levels - 1] = last
    for level in range(levels - 2, -1, -1):
        below = coefficient_refs[level]
        value = below[(levels - 1 - level) * rank:, :]
        for later in range(level + 1, levels):
            start = (later - level - 1) * rank
            value = value - dot_full(combined[later], below[start:start + rank, :])
        combined[level] = value
    value = aug_ref[levels * rank:, :] - dot_full(jnp.concatenate(combined, axis=1), aug_ref[:levels * rank, :])
    parts = [value[:, k * BLOCK:(k + 1) * BLOCK] for k in range(blocks)]
    for k in range(blocks - 1, 0, -1):
        moved = dot_full(parts[k], lower_ref[(k - 1) * BLOCK:k * BLOCK, :k * BLOCK])
        for j in range(k):
            parts[j] = parts[j] - moved[:, j * BLOCK:(j + 1) * BLOCK]
    solved = jnp.concatenate(parts, axis=1)
    positions = first_ref[0] + lax.broadcasted_iota(jnp.int32, (probes, width), 1)
    solve_ref[...] = solved[:probes]
    target_ref[...] = solved[probes:probes + 1]
    terms_ref[...] = jnp.sum(signs_of(seed_ref[...], positions) * solved[:probes], axis=0, keepdims=True)


def whole(count=1):
    return [pl.BlockSpec(memory_space=pltpu.VMEM)] * count


def scalars():
    return pl.BlockSpec(memory_space=pltpu.SMEM)


def shards(covariates, targets, noise_var, lengths, frequencies, phases, tree_order, probe_seeds):
    leaf_count = lax.axis_size("leaf")
    leaf_index = lax.axis_index("leaf")
    width = tree_order.shape[0]
    rank = phases.shape[1]
    probes = probe_seeds.shape[0]
    levels = leaf_count.bit_length() - 1
    tail = -(-(probes + 1) // 8) * 8
    packed = jnp.concatenate([covariates, targets[None, :], noise_var[None, :]], axis=0)
    pieces = [packed]
    for k in range(1, leaf_count):
        pieces.append(lax.ppermute(packed, "leaf", [(i, (i + k) % leaf_count) for i in range(leaf_count)]))
    gathered = jnp.concatenate(pieces, axis=1)
    owner = jnp.right_shift(tree_order, width.bit_length() - 1)
    place = jnp.bitwise_and(leaf_index - owner, leaf_count - 1) * width + jnp.bitwise_and(tree_order, width - 1)
    data = jnp.take(gathered, place, axis=1)
    first = jnp.stack([leaf_index * width, leaf_count + leaf_index]).astype(jnp.int32)
    seeds = probe_seeds[:, None]
    sizes = [(levels - level) * rank + tail for level in range(levels)]
    params = pltpu.CompilerParams(vmem_limit_bytes=VMEM_BYTES)
    lower, aug, sums = pl.pallas_call(
        functools.partial(leaf_kernel, levels),
        out_shape=(
            jax.ShapeDtypeStruct((width - BLOCK, width - BLOCK), f32),
            jax.ShapeDtypeStruct((levels * rank + tail, width), f32),
            jax.ShapeDtypeStruct((sum(sizes), rank), f32),
        ),
        in_specs=[scalars()] + whole(5),
        out_specs=tuple(whole(3)),
        scratch_shapes=[
            pltpu.VMEM((width + levels * rank + tail, width), f32),
            pltpu.VMEM((BLOCK, BLOCK), f32),
            pltpu.VMEM((BLOCK, BLOCK), f32),
        ],
        compiler_params=params,
        name="leaf",
    )(first, data, lengths[:, None], frequencies, phases, seeds)
    small = [pltpu.VMEM((rank, rank), f32), pltpu.VMEM((rank, rank), f32)]
    coefficients = []
    for height in range(1, levels):
        left = levels - height + 1
        other = partner_of(sums, "leaf", height - 1)
        coefficient, sums = pl.pallas_call(
            functools.partial(height_kernel, left, tail),
            out_shape=(
                jax.ShapeDtypeStruct((sizes[height - 1] - rank, rank), f32),
                jax.ShapeDtypeStruct((sum(sizes[height:]), rank), f32),
            ),
            in_specs=whole(2),
            out_specs=tuple(whole(2)),
            scratch_shapes=small,
            compiler_params=params,
            name=f"height_{height}",
        )(sums, other)
        coefficients.append(coefficient)
    other = partner_of(sums, "leaf", levels - 1)
    target_solve, probe_solves, terms = pl.pallas_call(
        functools.partial(final_kernel, levels, probes, tail),
        out_shape=(
            jax.ShapeDtypeStruct((1, width), f32),
            jax.ShapeDtypeStruct((probes, width), f32),
            jax.ShapeDtypeStruct((1, width), f32),
        ),
        in_specs=whole(2 + levels - 1 + 3) + [scalars()],
        out_specs=tuple(whole(3)),
        scratch_shapes=small,
        compiler_params=params,
        name="final",
    )(sums, other, *coefficients, lower, aug, seeds, first)
    for bit in range(lax.axis_size("probe").bit_length() - 1):
        terms = terms + partner_of(terms, "probe", bit)
    target_solve = target_solve[0]
    noise_grad = 0.5 * target_solve * target_solve - 0.5 * (terms[0] / PROBES)
    return (target_solve, probe_solves, noise_grad)


def solution(mesh):
    in_specs = (P(None, "leaf"), P("leaf"), P("leaf"), P(), P(), P(), P("leaf"), P("probe"))
    out_specs = (P("leaf"), P("probe", "leaf"), P("leaf"))
    return jax.shard_map(shards, mesh=mesh, in_specs=in_specs, out_specs=out_specs, check_vma=False)
```

```python
import functools
import math

import jax
import jax.numpy as jnp
from jax import lax
from jax.experimental import pallas as pl
from jax.experimental.pallas import tpu as pltpu
from jax.sharding import PartitionSpec as P

PROBES = 64
BLOCK = 256
SETTLED = 1.001
SHARES = ((3, 3, 3, 3, 3), (2, 2, 2, 2, 2))

f32 = jnp.float32
bf16 = jnp.bfloat16
highest = lax.Precision.HIGHEST
hash_first = 747796405
hash_second = -1403630843
hash_third = -2073254261
VMEM_BYTES = 40 * 1024 * 1024


def partner_of(block, axis, apart):
    count = lax.axis_size(axis)
    return lax.ppermute(block, axis, [(i, i ^ (1 << apart)) for i in range(count)])


def halves(x):
    high = x.astype(bf16)
    return high, (x - high.astype(f32)).astype(bf16)


def thirds(x):
    high = x.astype(bf16)
    rest = x - high.astype(f32)
    middle = rest.astype(bf16)
    return high, middle, (rest - middle.astype(f32)).astype(bf16)


NN = (((1,), (0,)), ((), ()))
NT = (((1,), (1,)), ((), ()))
TN = (((0,), (0,)), ((), ()))


def dot_one(a, b, dims=NN):
    return lax.dot_general(a, b, dims, preferred_element_type=f32)


def dot_three(a, b, dims=NN):
    a_high, a_low = halves(a)
    b_high, b_low = halves(b)
    return dot_one(a_high, b_high, dims) + (dot_one(a_high, b_low, dims) + dot_one(a_low, b_high, dims))


def dot_full(a, b, dims=NN):
    return lax.dot_general(a, b, dims, precision=highest, preferred_element_type=f32)


def unit(size):
    rows = lax.broadcasted_iota(jnp.int32, (size, size), 0)
    columns = lax.broadcasted_iota(jnp.int32, (size, size), 1)
    return rows == columns


def gain(ratio):
    reach = (ratio - 1.0) / (ratio + 1.0)
    return 2.0 / (2.0 - reach * reach)


def tighter(ratio):
    return (ratio + 1.0) * (ratio + 1.0) / (4.0 * ratio)


def no_work(count):
    pass


def inverse(matrix, low, residual, approx, other_work=no_work, share=(0, 0, 0, 0, 0)):
    size = matrix.shape[0]
    same = unit(size)
    high = jnp.max(jnp.sum(jnp.abs(matrix), axis=0, keepdims=True)) * 1.0001
    low = jnp.minimum(low, high) * 0.9999
    scale = 2.0 / (low + high)
    ratio = high / low
    c = gain(ratio)
    first = jnp.where(same, 1.0, 0.0) - scale * matrix
    residual[...] = c * dot_three(first, first) - jnp.where(same, c - 1.0, 0.0)
    approx[...] = (c * scale) * (first + jnp.where(same, 1.0, 0.0))
    ratio = tighter(ratio)
    other_work(share[0])

    def more(ratio):
        return tighter(ratio) > SETTLED

    def double(ratio):
        c = gain(ratio)
        e = residual[...]
        x = approx[...]
        squared = dot_three(e, e)
        moved = dot_three(x, e)
        residual[...] = c * squared - jnp.where(same, c - 1.0, 0.0)
        approx[...] = c * (x + moved)
        return tighter(ratio)

    for step in (1, 2):
        ratio = double(ratio)
        other_work(share[step])
    ratio = lax.while_loop(more, double, ratio)
    x = approx[...]
    x = gain(ratio) * (x + dot_three(x, residual[...]))
    other_work(share[3])
    left = jnp.where(same, 1.0, 0.0) - dot_full(x, matrix)
    other_work(share[4])
    return x + dot_three(left, x)


def cosine(x):
    turns = jnp.floor(x * (1.0 / math.pi) + 0.5)
    r = x - turns * 3.140625
    r = r - turns * 9.67502593994140625e-4
    r = r - turns * 1.509957990978376e-7
    odd = jnp.bitwise_and(turns.astype(jnp.int32), 1)
    s = r * r
    value = 1.0 / 479001600.0
    for term in (-1.0 / 3628800.0, 1.0 / 40320.0, -1.0 / 720.0, 1.0 / 24.0, -0.5, 1.0):
        value = value * s + term
    return jnp.where(odd == 1, -value, value)


def logical_right(x, by):
    return lax.shift_right_logical(x, jnp.full_like(x, by))


def signs_of(seeds, positions):
    mixed = seeds * jnp.int32(hash_first) + positions * jnp.int32(hash_second)
    mixed = jnp.bitwise_xor(mixed, logical_right(mixed, 15))
    mixed = mixed * jnp.int32(hash_third)
    mixed = jnp.bitwise_xor(mixed, logical_right(mixed, 13))
    parity = jnp.bitwise_and(logical_right(mixed, 11), jnp.full_like(mixed, 1))
    return (2 * parity - 1).astype(f32)


def fetch(half_and_covs, code, lane, near_ref, far_ref):
    chunks, lanes = code.shape
    half, covs = half_and_covs
    shape = (covs, lanes)
    codes = [jnp.broadcast_to(code[k:k + 1], shape) for k in range(chunks)]
    places = [jnp.broadcast_to(lane[k:k + 1], shape) for k in range(chunks)]
    down = lax.broadcasted_iota(jnp.int32, (chunks, lanes), 0)
    zero = jnp.zeros(shape, f32)

    def from_side(ref, side, totals):
        def from_piece(piece, totals):
            coords, targets, noise = [list(t) for t in totals]
            number = (side * half + piece) * chunks
            start = pl.multiple_of(piece * (chunks * (covs + 2)), 8)
            for c in range(chunks):
                source = ref[pl.ds(start + c * covs, covs), :]
                for k in range(chunks):
                    coords[k] = jnp.where(codes[k] == number + c, jnp.take_along_axis(source, places[k], axis=1), coords[k])
            for at, found in ((chunks * covs, targets), (chunks * (covs + 1), noise)):
                source = ref[pl.ds(start + at, chunks), :]
                for k in range(chunks):
                    found[k] = jnp.where(codes[k] == number + down, jnp.take_along_axis(source, places[k], axis=1), found[k])
            return tuple(coords), tuple(targets), tuple(noise)

        return lax.fori_loop(0, half, from_piece, totals)

    totals = ((zero,) * chunks,) * 3
    totals = from_side(far_ref, 1, from_side(near_ref, 0, totals))
    coords, targets, noise = totals
    return (
        jnp.concatenate(coords, axis=1),
        jnp.concatenate([jnp.sum(t, axis=0, keepdims=True) for t in targets], axis=1),
        jnp.concatenate([jnp.sum(t, axis=0, keepdims=True) for t in noise], axis=1),
    )


def down(row, count):
    shape = (count, row.shape[1])
    same = lax.broadcasted_iota(jnp.int32, shape, 0) == lax.broadcasted_iota(jnp.int32, shape, 1)
    return jnp.sum(jnp.where(same, jnp.broadcast_to(row, shape), jnp.zeros(shape, row.dtype)), axis=1, keepdims=True)


def early_kernel(levels, nodes, place_ref, whole_ref, real_ref, code_ref, lane_ref, scale_ref, wave_ref, sign_ref):
    chunks, lanes = code_ref.shape
    covs = scale_ref.shape[0]
    leaf = place_ref[0]
    half = 1 << (levels - 1)
    order = whole_ref[:chunks, :]
    owner = jnp.right_shift(order, (chunks * lanes).bit_length() - 1)
    chunk = jnp.bitwise_and(jnp.right_shift(order, lanes.bit_length() - 1), chunks - 1)
    across = jnp.bitwise_and(jnp.bitwise_xor(owner, leaf), 1)
    turn = jnp.bitwise_and(jnp.right_shift(jnp.bitwise_xor(leaf, across) - owner, 1), half - 1)
    code_ref[...] = (across * half + turn) * chunks + chunk
    lane_ref[...] = jnp.bitwise_and(order, lanes - 1)
    scale_ref[...] = jnp.broadcast_to(down(real_ref[nodes * (covs + 1):nodes * (covs + 1) + 1, :], covs), scale_ref.shape)
    rank = wave_ref.shape[2]
    at_row = lax.broadcasted_iota(jnp.int32, (8, rank), 0)
    for level in range(levels):
        node = jnp.right_shift((1 << levels) + leaf, level + 1) - 1
        fh, fm, fl = [p.astype(f32) for p in thirds(real_ref[pl.ds(pl.multiple_of(node * covs, covs), covs), :])]
        ph, pm, p_low = [p.astype(f32) for p in thirds(real_ref[pl.ds(nodes * covs + node, 1), :])]
        phases = jnp.where(at_row == 0, ph, jnp.where(at_row == 1, pm, jnp.where(at_row == 2, p_low, 0.0)))
        wave_ref[level] = jnp.concatenate([fh, fh, fm, fm, fh, fl, phases, jnp.zeros_like(phases)], axis=0)
    probes, width = sign_ref.shape
    positions = leaf * width + lax.broadcasted_iota(jnp.int32, (probes, width), 1)
    sign_ref[...] = signs_of(down(whole_ref[chunks:chunks + 1, :], probes), positions)


def leaf_kernel(levels, code_ref, lane_ref, scale_ref, wave_ref, sign_ref, near_ref, far_ref,
                lower_ref, aug_ref, first_ref, rest_ref, matrix, inverses, residual, approx):
    probes, width = sign_ref.shape
    rank = wave_ref.shape[2]
    covs = scale_ref.shape[0]
    blocks = width // BLOCK
    top = width + levels * rank
    coords, targets, noise = fetch((1 << (levels - 1), covs), code_ref[...], lane_ref[...], near_ref, far_ref)
    u = coords / scale_ref[:, :1]
    s = -0.5 * jnp.sum(u * u, axis=0, keepdims=True)
    rows = matrix.shape[0]
    h, m, l = [p.astype(f32) for p in thirds(u)]
    row = lax.broadcasted_iota(jnp.int32, (8, width), 0)
    ones = jnp.where(row < 3, 1.0, 0.0)
    same = unit(BLOCK)
    spans = [slice(k * BLOCK, (k + 1) * BLOCK) for k in range(blocks)]
    side_ranges = [(start, min(start + BLOCK, rows)) for start in range(width, rows, BLOCK)]
    leaf_ranges = [(k * BLOCK, (k + 1) * BLOCK) for k in range(blocks)]
    s_parts = [p.astype(f32) for p in thirds(s)]
    s_rows = jnp.where(row == 0, s_parts[0], jnp.where(row == 1, s_parts[1], jnp.where(row == 2, s_parts[2], 0.0)))
    left_points = jnp.concatenate([h, h, m, m, h, l, s_rows, ones], axis=0).astype(bf16)
    right_points = jnp.concatenate([h, m, h, m, l, h, ones, s_rows], axis=0).astype(bf16)
    basis_points = jnp.concatenate([h, m, h, m, l, h, ones, ones], axis=0).astype(bf16)

    def build(i, j):
        part = jnp.exp(dot_one(left_points[:, spans[i]], right_points[:, spans[j]], TN))
        if i == j:
            part = part + jnp.where(same, noise[:, spans[i]], 0.0)
        matrix[spans[i], spans[j]] = part

    def basis(level):
        angle = dot_one(wave_ref[level].astype(bf16), basis_points, TN)
        matrix[width + level * rank:width + (level + 1) * rank, :] = math.sqrt(2.0 / rank) * cosine(angle)

    def right_sides():
        matrix[top:top + probes, :] = sign_ref[...]
        matrix[top + probes:, :] = jnp.concatenate([targets, jnp.zeros((rows - top - probes - 1, width), f32)], axis=0)

    def weights_at(rows_of, k):
        start, end = rows_of
        if start < width:
            return lower_ref.at[start - BLOCK:end - BLOCK, spans[k]]
        return aug_ref.at[start - width:end - width, spans[k]]

    def weigh(rows_of, k):
        weights_at(rows_of, k)[...] = dot_full(matrix[rows_of[0]:rows_of[1], spans[k]], inverses[k % 2])

    def update(rows_of, j, k):
        here = slice(*rows_of)
        matrix[here, spans[j]] = matrix[here, spans[j]] - dot_full(weights_at(rows_of, k)[...], matrix[spans[j], spans[k]], NT)

    def add_up(level, k):
        many = min(2, levels - level)
        start = level * rank
        columns = matrix[width + start:width + start + many * rank, spans[k]]
        part = dot_full(aug_ref[start:, spans[k]], columns, NT)
        for next_to in range(many):
            column = level + next_to
            at = sum(rows - width - before * rank for before in range(1, column))
            count = rows - width - column * rank
            piece = part[next_to * rank:, next_to * rank:(next_to + 1) * rank]
            kept = (rest_ref if column else first_ref).at[at:at + count, :]
            kept[...] = piece if k == 0 else kept[...] + piece

    tasks, done, queue = {}, set(), []

    def add(key, call, after=()):
        tasks[key] = (call, after)
        queue.append(key)

    def run(key):
        if key not in done:
            done.add(key)
            call, after = tasks[key]
            for other in after:
                run(other)
            call()

    def other_work(count):
        while count and queue:
            key = queue.pop(0)
            if key not in done:
                run(key)
                count -= 1

    def ready(rows_of, j, k):
        if rows_of[0] < width:
            first = [("build", rows_of[0] // BLOCK, j)]
        else:
            first = [("basis", level) for level in range(levels)] + [("right",)]
        return first + [("update", rows_of, j, before) for before in range(k)]

    for j in range(blocks):
        for i in range(j, blocks):
            add(("build", i, j), functools.partial(build, i, j))
        if j == 0:
            for level in range(levels):
                add(("basis", level), functools.partial(basis, level))
            add(("right",), right_sides)
    for k in range(blocks):
        for key in ready(leaf_ranges[k], k, k):
            run(key)
        found = inverse(matrix[spans[k], spans[k]], jnp.min(noise[:, spans[k]]), residual, approx, other_work, SHARES[min(k, 1)])
        if k > 1:
            for key in tasks:
                if key[0] == "weigh" and key[2] == k - 2:
                    run(key)
        inverses[k % 2] = found
        ranges = leaf_ranges[k + 1:] + side_ranges
        for rows_of in ranges:
            add(("weigh", rows_of, k), functools.partial(weigh, rows_of, k), ready(rows_of, k, k))
        for j in range(k + 1, blocks):
            for rows_of in leaf_ranges[j:] + side_ranges:
                add(("update", rows_of, j, k), functools.partial(update, rows_of, j, k),
                    ready(rows_of, j, 0) + ready(leaf_ranges[j], k, k) + [("weigh", rows_of, k)])
        for level in range(0, levels, 2):
            add(("sum", level, k), functools.partial(add_up, level, k),
                [("weigh", rows_of, k) for rows_of in side_ranges]
                + [key for rows_of in side_ranges for key in ready(rows_of, k, k)])
    other_work(len(queue))


def eliminate(own, other, rank, residual, approx):
    total = own + other
    capacitance = total[:rank] + jnp.where(unit(rank), 1.0, 0.0)
    return total, dot_full(total[rank:], inverse(capacitance, jnp.float32(1.0), residual, approx))


def height_kernel(own_ref, other_ref, coefficient_ref, total_ref, residual, approx):
    total, coefficients = eliminate(own_ref[...], other_ref[...], own_ref.shape[1], residual, approx)
    coefficient_ref[...] = coefficients
    total_ref[...] = total[own_ref.shape[1]:]


def reduce_kernel(left, coefficient_ref, total_ref, own_ref, other_ref, *out_refs):
    rank = own_ref.shape[1]
    at = to = 0
    for level in range(1, left):
        start = (level - 1) * rank
        size = coefficient_ref.shape[0] - start
        value = own_ref[at:at + size, :] + other_ref[at:at + size, :] - dot_full(
            coefficient_ref[start:, :], total_ref[start:start + rank, :], NT)
        if level == 1:
            out_refs[0][...] = value
        else:
            out_refs[1][to:to + size, :] = value
            to += size
        at += size


def back_kernel(lower_ref, aug_ref, solved_ref):
    width = aug_ref.shape[1]
    spans = [slice(k * BLOCK, (k + 1) * BLOCK) for k in range(width // BLOCK)]
    for k in range(len(spans) - 1, -1, -1):
        value = aug_ref[:, spans[k]]
        for j in range(k + 1, len(spans)):
            value = value - dot_full(solved_ref[:, spans[j]], lower_ref[(j - 1) * BLOCK:j * BLOCK, spans[k]])
        solved_ref[:, spans[k]] = value


def apply_kernel(coefficient_ref, solved_ref, rest_ref):
    rank = coefficient_ref.shape[1]
    rest_ref[...] = solved_ref[rank:, :] - dot_full(coefficient_ref[...], solved_ref[:rank, :])


def final_kernel(own_ref, other_ref, solved_ref, sign_ref, target_ref, solve_ref, terms_ref, residual, approx):
    rank = own_ref.shape[1]
    probes = sign_ref.shape[0]
    _, last = eliminate(own_ref[...], other_ref[...], rank, residual, approx)
    solved = solved_ref[rank:, :] - dot_full(last, solved_ref[:rank, :])
    solve_ref[...] = solved[:probes]
    target_ref[...] = solved[probes:probes + 1]
    terms_ref[...] = jnp.sum(sign_ref[...] * solved[:probes], axis=0, keepdims=True)


def whole(count=1):
    return [pl.BlockSpec(memory_space=pltpu.VMEM)] * count


def scalars():
    return pl.BlockSpec(memory_space=pltpu.SMEM)


def shards(covariates, targets, noise_var, lengths, frequencies, phases, tree_order, probe_seeds):
    leaf_count = lax.axis_size("leaf")
    leaf_index = lax.axis_index("leaf")
    width = tree_order.shape[0]
    rank = phases.shape[1]
    probes = probe_seeds.shape[0]
    levels = leaf_count.bit_length() - 1
    tail = -(-(probes + 1) // 8) * 8
    lanes = 128
    chunks = width // lanes
    covs = covariates.shape[0]
    piece = jnp.concatenate(
        [
            covariates.reshape(covs, chunks, lanes).transpose(1, 0, 2).reshape(chunks * covs, lanes),
            targets.reshape(chunks, lanes),
            noise_var.reshape(chunks, lanes),
        ],
        axis=0,
    )
    piece = lax.optimization_barrier(piece)
    pieces = [piece]
    for k in range(2, leaf_count, 2):
        pieces.append(lax.ppermute(piece, "leaf", [(i, (i + k) % leaf_count) for i in range(leaf_count)]))
    near = jnp.concatenate(pieces, axis=0)
    place = leaf_index[None].astype(jnp.int32)
    sizes = [(levels - level) * rank + tail for level in range(levels)]
    params = pltpu.CompilerParams(vmem_limit_bytes=VMEM_BYTES)
    nodes = phases.shape[0]
    integers = jnp.concatenate([tree_order.reshape(chunks, lanes), jnp.pad(probe_seeds, (0, lanes - probes))[None]], axis=0)
    reals = jnp.concatenate([frequencies.reshape(nodes * covs, rank), phases, jnp.pad(lengths, (0, rank - covs))[None]], axis=0)
    code, lane, scale, waves, signs = pl.pallas_call(
        functools.partial(early_kernel, levels, nodes),
        out_shape=(
            jax.ShapeDtypeStruct((chunks, lanes), jnp.int32),
            jax.ShapeDtypeStruct((chunks, lanes), jnp.int32),
            jax.ShapeDtypeStruct((covs, lanes), f32),
            jax.ShapeDtypeStruct((levels, 8 * covs, rank), f32),
            jax.ShapeDtypeStruct((probes, width), f32),
        ),
        in_specs=[scalars()] + whole(2),
        out_specs=tuple(whole(5)),
        compiler_params=params,
        name="early",
    )(place, integers, reals)
    near, code, lane, scale, waves, signs = lax.optimization_barrier((near, code, lane, scale, waves, signs))
    far = partner_of(near, "leaf", 0)
    side = levels * rank + tail
    lower, aug, first, later = pl.pallas_call(
        functools.partial(leaf_kernel, levels),
        out_shape=(
            jax.ShapeDtypeStruct((width - BLOCK, width - BLOCK), f32),
            jax.ShapeDtypeStruct((side, width), f32),
            jax.ShapeDtypeStruct((sizes[0], rank), f32),
            jax.ShapeDtypeStruct((sum(sizes[1:]), rank), f32),
        ),
        in_specs=whole(7),
        out_specs=tuple(whole(4)),
        scratch_shapes=[
            pltpu.VMEM((width + side, width), f32),
            pltpu.VMEM((2, BLOCK, BLOCK), f32),
            pltpu.VMEM((BLOCK, BLOCK), f32),
            pltpu.VMEM((BLOCK, BLOCK), f32),
        ],
        compiler_params=params,
        name="leaf",
    )(code, lane, scale, waves, signs, near, far)
    small = [pltpu.VMEM((rank, rank), f32), pltpu.VMEM((rank, rank), f32)]
    solved = pl.pallas_call(
        back_kernel,
        out_shape=jax.ShapeDtypeStruct((side, width), f32),
        in_specs=whole(2),
        out_specs=whole()[0],
        compiler_params=params,
        cost_estimate=pl.CostEstimate(flops=12 * side * width * width // 2, bytes_accessed=0, transcendentals=0),
        name="back",
    )(lower, aug)
    for height in range(1, levels):
        left = levels - height + 1
        other_first = partner_of(first, "leaf", height - 1)
        other_later = partner_of(later, "leaf", height - 1)
        other_first, solved = lax.optimization_barrier((other_first, solved))
        rest = side - height * rank
        coefficient, total = pl.pallas_call(
            height_kernel,
            out_shape=(jax.ShapeDtypeStruct((rest, rank), f32), jax.ShapeDtypeStruct((rest, rank), f32)),
            in_specs=whole(2),
            out_specs=tuple(whole(2)),
            scratch_shapes=small,
            compiler_params=params,
            name=f"height_{height}",
        )(first, other_first)
        outs = [jax.ShapeDtypeStruct((sizes[height], rank), f32)]
        if left > 2:
            outs.append(jax.ShapeDtypeStruct((sum(sizes[height + 1:]), rank), f32))
        found = pl.pallas_call(
            functools.partial(reduce_kernel, left),
            out_shape=tuple(outs),
            in_specs=whole(4),
            out_specs=tuple(whole(len(outs))),
            compiler_params=params,
            name=f"reduce_{height}",
        )(coefficient, total, later, other_later)
        first, later = found[0], found[-1]
        solved = pl.pallas_call(
            apply_kernel,
            out_shape=jax.ShapeDtypeStruct((rest, width), f32),
            in_specs=whole(2),
            out_specs=whole()[0],
            compiler_params=params,
            cost_estimate=pl.CostEstimate(flops=12 * rest * rank * width, bytes_accessed=0, transcendentals=0),
            name=f"apply_{height}",
        )(coefficient, solved)
    other = partner_of(first, "leaf", levels - 1)
    target_solve, probe_solves, terms = pl.pallas_call(
        final_kernel,
        out_shape=(
            jax.ShapeDtypeStruct((1, width), f32),
            jax.ShapeDtypeStruct((probes, width), f32),
            jax.ShapeDtypeStruct((1, width), f32),
        ),
        in_specs=whole(4),
        out_specs=tuple(whole(3)),
        scratch_shapes=small,
        compiler_params=params,
        name="final",
    )(first, other, solved, signs)
    probe_count = lax.axis_size("probe")
    shared = [terms] + [
        lax.ppermute(terms, "probe", [(i, (i + k) % probe_count) for i in range(probe_count)]) for k in range(1, probe_count)
    ]
    target_solve = target_solve[0]
    estimate = functools.reduce(jnp.add, [t[0] for t in shared]) / PROBES
    noise_grad = 0.5 * target_solve * target_solve - 0.5 * estimate
    return (target_solve, probe_solves, noise_grad)


def solution(mesh):
    in_specs = (P(None, "leaf"), P("leaf"), P("leaf"), P(), P(), P(), P("leaf"), P("probe"))
    out_specs = (P("leaf"), P("probe", "leaf"), P("leaf"))
    return jax.shard_map(shards, mesh=mesh, in_specs=in_specs, out_specs=out_specs, check_vma=False)
```

```python
import functools
import math

import jax
import jax.numpy as jnp
from jax import lax
from jax.experimental import pallas as pl
from jax.experimental.pallas import tpu as pltpu
from jax.sharding import PartitionSpec as P

PROBES = 64
BLOCK = 256
SETTLED = 1.001
TAME = 256.0
SHARES = ((3, 3, 3, 3, 3), (2, 2, 2, 2, 2))

f32 = jnp.float32
bf16 = jnp.bfloat16
highest = lax.Precision.HIGHEST
hash_first = 747796405
hash_second = -1403630843
hash_third = -2073254261
VMEM_BYTES = 40 * 1024 * 1024


def partner_of(block, axis, apart):
    count = lax.axis_size(axis)
    return lax.ppermute(block, axis, [(i, i ^ (1 << apart)) for i in range(count)])


def halves(x):
    high = x.astype(bf16)
    return high, (x - high.astype(f32)).astype(bf16)


def thirds(x):
    high = x.astype(bf16)
    rest = x - high.astype(f32)
    middle = rest.astype(bf16)
    return high, middle, (rest - middle.astype(f32)).astype(bf16)


NN = (((1,), (0,)), ((), ()))
NT = (((1,), (1,)), ((), ()))
TN = (((0,), (0,)), ((), ()))


def dot_one(a, b, dims=NN):
    return lax.dot_general(a, b, dims, preferred_element_type=f32)


def dot_three(a, b, dims=NN):
    a_high, a_low = halves(a)
    b_high, b_low = halves(b)
    return dot_one(a_high, b_high, dims) + (dot_one(a_high, b_low, dims) + dot_one(a_low, b_high, dims))


def dot_full(a, b, dims=NN):
    return lax.dot_general(a, b, dims, precision=highest, preferred_element_type=f32)


def unit(size):
    rows = lax.broadcasted_iota(jnp.int32, (size, size), 0)
    columns = lax.broadcasted_iota(jnp.int32, (size, size), 1)
    return rows == columns


def gain(ratio):
    reach = (ratio - 1.0) / (ratio + 1.0)
    return 2.0 / (2.0 - reach * reach)


def tighter(ratio):
    return (ratio + 1.0) * (ratio + 1.0) / (4.0 * ratio)


def no_work(count):
    pass


def inverse(matrix, low, residual, approx, other_work=no_work, share=(0, 0, 0, 0, 0)):
    size = matrix.shape[0]
    same = unit(size)
    high = jnp.max(jnp.sum(jnp.abs(matrix), axis=0, keepdims=True)) * 1.0001
    low = jnp.minimum(low, high) * 0.9999
    scale = 2.0 / (low + high)
    ratio = high / low
    c = gain(ratio)
    first = jnp.where(same, 1.0, 0.0) - scale * matrix
    residual[...] = c * dot_three(first, first) - jnp.where(same, c - 1.0, 0.0)
    approx[...] = (c * scale) * (first + jnp.where(same, 1.0, 0.0))
    ratio = tighter(ratio)
    other_work(share[0])

    def more(ratio):
        return tighter(ratio) > SETTLED

    def double(ratio):
        c = gain(ratio)
        e = residual[...]
        x = approx[...]
        squared = dot_three(e, e)
        moved = dot_three(x, e)
        residual[...] = c * squared - jnp.where(same, c - 1.0, 0.0)
        approx[...] = c * (x + moved)
        return tighter(ratio)

    for step in (1, 2):
        ratio = double(ratio)
        other_work(share[step])
    ratio = lax.while_loop(more, double, ratio)
    x = approx[...]
    x = gain(ratio) * (x + dot_three(x, residual[...]))
    other_work(share[3])
    left = jnp.where(same, 1.0, 0.0) - dot_full(x, matrix)
    other_work(share[4])
    return x + dot_three(left, x)


def cosine(x):
    turns = jnp.floor(x * (1.0 / math.pi) + 0.5)
    r = x - turns * 3.140625
    r = r - turns * 9.67502593994140625e-4
    r = r - turns * 1.509957990978376e-7
    odd = jnp.bitwise_and(turns.astype(jnp.int32), 1)
    s = r * r
    value = 1.0 / 479001600.0
    for term in (-1.0 / 3628800.0, 1.0 / 40320.0, -1.0 / 720.0, 1.0 / 24.0, -0.5, 1.0):
        value = value * s + term
    return jnp.where(odd == 1, -value, value)


def logical_right(x, by):
    return lax.shift_right_logical(x, jnp.full_like(x, by))


def signs_of(seeds, positions):
    mixed = seeds * jnp.int32(hash_first) + positions * jnp.int32(hash_second)
    mixed = jnp.bitwise_xor(mixed, logical_right(mixed, 15))
    mixed = mixed * jnp.int32(hash_third)
    mixed = jnp.bitwise_xor(mixed, logical_right(mixed, 13))
    parity = jnp.bitwise_and(logical_right(mixed, 11), jnp.full_like(mixed, 1))
    return (2 * parity - 1).astype(f32)


def fetch(side, code_ref, lane_ref, ref, totals):
    chunks, lanes = code_ref.shape
    covs = totals[0][0].shape[0]
    size = chunks * (covs + 2)
    pieces = ref.shape[0] // size
    shape = (covs, lanes)
    codes = [jnp.broadcast_to(code_ref[k:k + 1, :], shape) for k in range(chunks)]
    places = [jnp.broadcast_to(lane_ref[k:k + 1, :], shape) for k in range(chunks)]
    rows = lax.broadcasted_iota(jnp.int32, (chunks, lanes), 0)

    def from_piece(piece, totals):
        coords, targets, noise = [list(t) for t in totals]
        number = (side * pieces + piece) * chunks
        start = pl.multiple_of(piece * size, 8)
        for c in range(chunks):
            source = ref[pl.ds(start + c * covs, covs), :]
            for k in range(chunks):
                coords[k] = jnp.where(codes[k] == number + c, jnp.take_along_axis(source, places[k], axis=1), coords[k])
        for at, found in ((chunks * covs, targets), (chunks * (covs + 1), noise)):
            source = ref[pl.ds(start + at, chunks), :]
            for k in range(chunks):
                found[k] = jnp.where(codes[k] == number + rows, jnp.take_along_axis(source, places[k], axis=1), found[k])
        return tuple(coords), tuple(targets), tuple(noise)

    return lax.fori_loop(0, pieces, from_piece, totals)


def near_kernel(code_ref, lane_ref, near_ref, point_ref):
    chunks, lanes = code_ref.shape
    totals = ((jnp.zeros((point_ref.shape[0] // (3 * chunks), lanes), f32),) * chunks,) * 3
    found = fetch(0, code_ref, lane_ref, near_ref, totals)
    point_ref[...] = jnp.concatenate([t for part in found for t in part], axis=0)


def points_of(code_ref, lane_ref, point_ref, far_ref):
    chunks = code_ref.shape[0]
    covs = point_ref.shape[0] // (3 * chunks)
    parts = [point_ref[k * covs:(k + 1) * covs, :] for k in range(3 * chunks)]
    totals = tuple(tuple(parts[k * chunks:(k + 1) * chunks]) for k in range(3))
    coords, targets, noise = fetch(1, code_ref, lane_ref, far_ref, totals)
    return (
        jnp.concatenate(coords, axis=1),
        jnp.concatenate([jnp.sum(t, axis=0, keepdims=True) for t in targets], axis=1),
        jnp.concatenate([jnp.sum(t, axis=0, keepdims=True) for t in noise], axis=1),
    )


def down(row, count):
    shape = (count, row.shape[1])
    same = lax.broadcasted_iota(jnp.int32, shape, 0) == lax.broadcasted_iota(jnp.int32, shape, 1)
    return jnp.sum(jnp.where(same, jnp.broadcast_to(row, shape), jnp.zeros(shape, row.dtype)), axis=1, keepdims=True)


def early_kernel(levels, nodes, place_ref, whole_ref, real_ref, code_ref, lane_ref, scale_ref, wave_ref, sign_ref):
    chunks, lanes = code_ref.shape
    covs = scale_ref.shape[0]
    leaf = place_ref[0]
    half = 1 << (levels - 1)
    order = whole_ref[:chunks, :]
    owner = jnp.right_shift(order, (chunks * lanes).bit_length() - 1)
    chunk = jnp.bitwise_and(jnp.right_shift(order, lanes.bit_length() - 1), chunks - 1)
    across = jnp.bitwise_and(jnp.bitwise_xor(owner, leaf), 1)
    turn = jnp.bitwise_and(jnp.right_shift(jnp.bitwise_xor(leaf, across) - owner, 1), half - 1)
    code_ref[...] = (across * half + turn) * chunks + chunk
    lane_ref[...] = jnp.bitwise_and(order, lanes - 1)
    scale_ref[...] = jnp.broadcast_to(down(real_ref[nodes * (covs + 1):nodes * (covs + 1) + 1, :], covs), scale_ref.shape)
    rank = wave_ref.shape[2]
    at_row = lax.broadcasted_iota(jnp.int32, (8, rank), 0)
    for level in range(levels):
        node = jnp.right_shift((1 << levels) + leaf, level + 1) - 1
        fh, fm, fl = [p.astype(f32) for p in thirds(real_ref[pl.ds(pl.multiple_of(node * covs, covs), covs), :])]
        ph, pm, p_low = [p.astype(f32) for p in thirds(real_ref[pl.ds(nodes * covs + node, 1), :])]
        phases = jnp.where(at_row == 0, ph, jnp.where(at_row == 1, pm, jnp.where(at_row == 2, p_low, 0.0)))
        wave_ref[level] = jnp.concatenate([fh, fh, fm, fm, fh, fl, phases, jnp.zeros_like(phases)], axis=0)
    probes, width = sign_ref.shape
    positions = leaf * width + lax.broadcasted_iota(jnp.int32, (probes, width), 1)
    sign_ref[...] = signs_of(down(whole_ref[chunks:chunks + 1, :], probes), positions)


def leaf_kernel(levels, code_ref, lane_ref, scale_ref, wave_ref, sign_ref, point_ref, far_ref,
                lower_ref, aug_ref, first_ref, rest_ref, matrix, inverses, residual, approx,
                left_points, right_points, basis_points):
    probes, width = sign_ref.shape
    rank = wave_ref.shape[2]
    covs = scale_ref.shape[0]
    blocks = width // BLOCK
    top = width + levels * rank
    coords, targets, noise = points_of(code_ref, lane_ref, point_ref, far_ref)
    u = coords / scale_ref[:, :1]
    s = -0.5 * jnp.sum(u * u, axis=0, keepdims=True)
    rows = matrix.shape[0]
    h, m, l = [p.astype(f32) for p in thirds(u)]
    row = lax.broadcasted_iota(jnp.int32, (8, width), 0)
    ones = jnp.where(row < 3, 1.0, 0.0)
    same = unit(BLOCK)
    spans = [slice(k * BLOCK, (k + 1) * BLOCK) for k in range(blocks)]
    side_ranges = [(start, min(start + BLOCK, rows)) for start in range(width, rows, BLOCK)]
    leaf_ranges = [(k * BLOCK, (k + 1) * BLOCK) for k in range(blocks)]
    s_parts = [p.astype(f32) for p in thirds(s)]
    s_rows = jnp.where(row == 0, s_parts[0], jnp.where(row == 1, s_parts[1], jnp.where(row == 2, s_parts[2], 0.0)))
    left_points[...] = jnp.concatenate([h, h, m, m, h, l, s_rows, ones], axis=0).astype(bf16)
    right_points[...] = jnp.concatenate([h, m, h, m, l, h, ones, s_rows], axis=0).astype(bf16)
    basis_points[...] = jnp.concatenate([h, m, h, m, l, h, ones, ones], axis=0).astype(bf16)

    def build(i, j):
        part = jnp.exp(dot_one(left_points[:, spans[i]], right_points[:, spans[j]], TN))
        if i == j:
            part = part + jnp.where(same, noise[:, spans[i]], 0.0)
        matrix[spans[i], spans[j]] = part

    def basis(level):
        angle = dot_one(wave_ref[level].astype(bf16), basis_points[...], TN)
        matrix[width + level * rank:width + (level + 1) * rank, :] = math.sqrt(2.0 / rank) * cosine(angle)

    def right_sides():
        matrix[top:top + probes, :] = sign_ref[...]
        matrix[top + probes:, :] = jnp.concatenate([targets, jnp.zeros((rows - top - probes - 1, width), f32)], axis=0)

    def weights_at(rows_of, k):
        start, end = rows_of
        if start < width:
            return lower_ref.at[start - BLOCK:end - BLOCK, spans[k]]
        return aug_ref.at[start - width:end - width, spans[k]]

    def all_steps(dot):
        def weigh(rows_of, k):
            weights_at(rows_of, k)[...] = dot(matrix[rows_of[0]:rows_of[1], spans[k]], inverses[k % 2])

        def update(rows_of, j, k):
            here = slice(*rows_of)
            matrix[here, spans[j]] = matrix[here, spans[j]] - dot(weights_at(rows_of, k)[...], matrix[spans[j], spans[k]], NT)

        def add_up(level, k):
            many = min(2, levels - level)
            start = level * rank
            columns = matrix[width + start:width + start + many * rank, spans[k]]
            part = dot_three(aug_ref[start:, spans[k]], columns, NT)
            for next_to in range(many):
                column = level + next_to
                at = sum(rows - width - before * rank for before in range(1, column))
                count = rows - width - column * rank
                piece = part[next_to * rank:, next_to * rank:(next_to + 1) * rank]
                kept = (rest_ref if column else first_ref).at[at:at + count, :]
                kept[...] = piece if k == 0 else kept[...] + piece

        tasks, done, queue = {}, set(), []

        def add(key, call, after=()):
            tasks[key] = (call, after)
            queue.append(key)

        def run(key):
            if key not in done:
                done.add(key)
                call, after = tasks[key]
                for other in after:
                    run(other)
                call()

        def other_work(count):
            while count and queue:
                key = queue.pop(0)
                if key not in done:
                    run(key)
                    count -= 1

        def ready(rows_of, j, k):
            if rows_of[0] < width:
                first = [("build", rows_of[0] // BLOCK, j)]
            else:
                first = [("basis", level) for level in range(levels)] + [("right",)]
            return first + [("update", rows_of, j, before) for before in range(k)]

        for j in range(blocks):
            done.add(("build", j, j))
            for i in range(j + 1, blocks):
                add(("build", i, j), functools.partial(build, i, j))
            if j == 0:
                for level in range(levels):
                    add(("basis", level), functools.partial(basis, level))
                add(("right",), right_sides)
        for k in range(blocks):
            for key in ready(leaf_ranges[k], k, k):
                run(key)
            found = inverse(matrix[spans[k], spans[k]], jnp.min(noise[:, spans[k]]), residual, approx, other_work, SHARES[min(k, 1)])
            if k > 1:
                for key in tasks:
                    if key[0] == "weigh" and key[2] == k - 2:
                        run(key)
            inverses[k % 2] = found
            ranges = leaf_ranges[k + 1:] + side_ranges
            for rows_of in ranges:
                add(("weigh", rows_of, k), functools.partial(weigh, rows_of, k), ready(rows_of, k, k))
            for j in range(k + 1, blocks):
                for rows_of in leaf_ranges[j:] + side_ranges:
                    add(("update", rows_of, j, k), functools.partial(update, rows_of, j, k),
                        ready(rows_of, j, 0) + ready(leaf_ranges[j], k, k) + [("weigh", rows_of, k)])
            for level in range(0, levels, 2):
                add(("sum", level, k), functools.partial(add_up, level, k),
                    [("weigh", rows_of, k) for rows_of in side_ranges]
                    + [key for rows_of in side_ranges for key in ready(rows_of, k, k)])
        other_work(len(queue))

    def all_full():
        side = rows - width
        chunk = max(c for c in range(8, BLOCK + 1, 8) if side % c == 0)

        def span_of(k, size=BLOCK, start=0):
            return pl.ds(pl.multiple_of(start + k * size, 8 if size < BLOCK else BLOCK), size)

        def rebuild(i, carry):
            part = jnp.exp(dot_one(left_points[:, span_of(i)], right_points[...], TN))
            row = i * BLOCK + lax.broadcasted_iota(jnp.int32, (BLOCK, width), 0)
            matrix[span_of(i), :] = part + jnp.where(row == lax.broadcasted_iota(jnp.int32, (BLOCK, width), 1), noise, 0.0)
            return carry

        def wave(level, carry):
            angle = dot_one(wave_ref[level].astype(bf16), basis_points[...], TN)
            matrix[pl.ds(pl.multiple_of(width + level * rank, rank), rank), :] = math.sqrt(2.0 / rank) * cosine(angle)
            return carry

        def step(k, carry):
            here = span_of(k)
            inverses[0] = inverse(matrix[here, here], jnp.min(noise), residual, approx)

            def weigh_leaf(r, carry):
                lower_ref[span_of(r - 1), here] = dot_full(matrix[span_of(r), here], inverses[0])
                return carry

            def weigh_side(r, carry):
                aug_ref[span_of(r, chunk), here] = dot_full(matrix[span_of(r, chunk, width), here], inverses[0])
                return carry

            def column(j, carry):
                there = span_of(j)

                def update_leaf(r, carry):
                    matrix[span_of(r), there] -= dot_full(lower_ref[span_of(r - 1), here], matrix[there, here], NT)
                    return carry

                def update_side(r, carry):
                    at = span_of(r, chunk, width)
                    matrix[at, there] -= dot_full(aug_ref[span_of(r, chunk), here], matrix[there, here], NT)
                    return carry

                lax.fori_loop(j, blocks, update_leaf, 0)
                return lax.fori_loop(0, side // chunk, update_side, carry)

            lax.fori_loop(k + 1, blocks, weigh_leaf, 0)
            lax.fori_loop(0, side // chunk, weigh_side, 0)
            return lax.fori_loop(k + 1, blocks, column, carry)

        lax.fori_loop(0, blocks, rebuild, 0)
        lax.fori_loop(0, levels, wave, 0)
        right_sides()
        lax.fori_loop(0, blocks, step, 0)
        for level in range(levels):
            at = sum(side - before * rank for before in range(1, level))
            kept = rest_ref if level else first_ref

            def add_rows(r, carry):
                kept[span_of(r, 8, at), :] = dot_full(
                    aug_ref[span_of(r, 8, level * rank), :], matrix[width + level * rank:width + (level + 1) * rank, :], NT)
                return carry

            lax.fori_loop(0, (side - level * rank) // 8, add_rows, 0)

    total = jnp.zeros((), f32)
    for k in range(blocks):
        build(k, k)
        total = total + jnp.max(jnp.sum(matrix[spans[k], spans[k]], axis=0, keepdims=True))
    tame = total <= TAME * jnp.min(noise)

    all_steps(dot_three)

    @pl.when(jnp.logical_not(tame))
    def _():
        all_full()


def eliminate(own, other, rank, residual, approx):
    total = own + other
    capacitance = total[:rank] + jnp.where(unit(rank), 1.0, 0.0)
    return total, dot_full(total[rank:], inverse(capacitance, jnp.float32(1.0), residual, approx))


def height_kernel(own_ref, other_ref, coefficient_ref, total_ref, residual, approx):
    total, coefficients = eliminate(own_ref[...], other_ref[...], own_ref.shape[1], residual, approx)
    coefficient_ref[...] = coefficients
    total_ref[...] = total[own_ref.shape[1]:]


def reduce_kernel(left, coefficient_ref, total_ref, own_ref, other_ref, *out_refs):
    rank = own_ref.shape[1]
    at = to = 0
    for level in range(1, left):
        start = (level - 1) * rank
        size = coefficient_ref.shape[0] - start
        value = own_ref[at:at + size, :] + other_ref[at:at + size, :] - dot_full(
            coefficient_ref[start:, :], total_ref[start:start + rank, :], NT)
        if level == 1:
            out_refs[0][...] = value
        else:
            out_refs[1][to:to + size, :] = value
            to += size
        at += size


def back_kernel(lower_ref, aug_ref, solved_ref):
    width = aug_ref.shape[1]
    spans = [slice(k * BLOCK, (k + 1) * BLOCK) for k in range(width // BLOCK)]
    for k in range(len(spans) - 1, -1, -1):
        value = aug_ref[:, spans[k]]
        for j in range(k + 1, len(spans)):
            value = value - dot_full(solved_ref[:, spans[j]], lower_ref[(j - 1) * BLOCK:j * BLOCK, spans[k]])
        solved_ref[:, spans[k]] = value


def apply_kernel(coefficient_ref, solved_ref, rest_ref):
    rank = coefficient_ref.shape[1]
    rest_ref[...] = solved_ref[rank:, :] - dot_full(coefficient_ref[...], solved_ref[:rank, :])


def final_kernel(own_ref, other_ref, solved_ref, sign_ref, target_ref, solve_ref, terms_ref, all_ref, residual, approx):
    rank = own_ref.shape[1]
    probes = sign_ref.shape[0]
    _, last = eliminate(own_ref[...], other_ref[...], rank, residual, approx)
    solved = solved_ref[rank:, :] - dot_full(last, solved_ref[:rank, :])
    solve_ref[...] = solved[:probes]
    target = solved[probes:probes + 1]
    target_ref[...] = target
    terms = (-0.5 / PROBES) * jnp.sum(sign_ref[...] * solved[:probes], axis=0, keepdims=True)
    terms_ref[...] = terms
    all_ref[...] = 0.5 * target * target + terms


def whole(count=1):
    return [pl.BlockSpec(memory_space=pltpu.VMEM)] * count


def scalars():
    return pl.BlockSpec(memory_space=pltpu.SMEM)


def shards(covariates, targets, noise_var, lengths, frequencies, phases, tree_order, probe_seeds):
    leaf_count = lax.axis_size("leaf")
    leaf_index = lax.axis_index("leaf")
    width = tree_order.shape[0]
    rank = phases.shape[1]
    probes = probe_seeds.shape[0]
    levels = leaf_count.bit_length() - 1
    tail = -(-(probes + 1) // 8) * 8
    lanes = 128
    chunks = width // lanes
    covs = covariates.shape[0]
    piece = jnp.concatenate(
        [
            covariates.reshape(covs, chunks, lanes).transpose(1, 0, 2).reshape(chunks * covs, lanes),
            targets.reshape(chunks, lanes),
            noise_var.reshape(chunks, lanes),
        ],
        axis=0,
    )
    piece = lax.optimization_barrier(piece)
    pieces = [piece]
    for k in range(2, leaf_count, 2):
        pieces.append(lax.ppermute(piece, "leaf", [(i, (i + k) % leaf_count) for i in range(leaf_count)]))
    near = jnp.concatenate(pieces, axis=0)
    place = leaf_index[None].astype(jnp.int32)
    sizes = [(levels - level) * rank + tail for level in range(levels)]
    params = pltpu.CompilerParams(vmem_limit_bytes=VMEM_BYTES)
    nodes = phases.shape[0]
    integers = jnp.concatenate([tree_order.reshape(chunks, lanes), jnp.pad(probe_seeds, (0, lanes - probes))[None]], axis=0)
    reals = jnp.concatenate([frequencies.reshape(nodes * covs, rank), phases, jnp.pad(lengths, (0, rank - covs))[None]], axis=0)
    code, lane, scale, waves, signs = pl.pallas_call(
        functools.partial(early_kernel, levels, nodes),
        out_shape=(
            jax.ShapeDtypeStruct((chunks, lanes), jnp.int32),
            jax.ShapeDtypeStruct((chunks, lanes), jnp.int32),
            jax.ShapeDtypeStruct((covs, lanes), f32),
            jax.ShapeDtypeStruct((levels, 8 * covs, rank), f32),
            jax.ShapeDtypeStruct((probes, width), f32),
        ),
        in_specs=[scalars()] + whole(2),
        out_specs=tuple(whole(5)),
        compiler_params=params,
        name="early",
    )(place, integers, reals)
    near, code, lane, scale, waves, signs = lax.optimization_barrier((near, code, lane, scale, waves, signs))
    far = partner_of(near, "leaf", 0)
    points = pl.pallas_call(
        near_kernel,
        out_shape=jax.ShapeDtypeStruct((3 * chunks * covs, lanes), f32),
        in_specs=whole(3),
        out_specs=whole()[0],
        compiler_params=params,
        cost_estimate=pl.CostEstimate(flops=10**9, bytes_accessed=0, transcendentals=0),
        name="near",
    )(code, lane, near)
    far, points = lax.optimization_barrier((far, points))
    side = levels * rank + tail
    lower, aug, first, later = pl.pallas_call(
        functools.partial(leaf_kernel, levels),
        out_shape=(
            jax.ShapeDtypeStruct((width - BLOCK, width - BLOCK), f32),
            jax.ShapeDtypeStruct((side, width), f32),
            jax.ShapeDtypeStruct((sizes[0], rank), f32),
            jax.ShapeDtypeStruct((sum(sizes[1:]), rank), f32),
        ),
        in_specs=whole(7),
        out_specs=tuple(whole(4)),
        scratch_shapes=[
            pltpu.VMEM((width + side, width), f32),
            pltpu.VMEM((2, BLOCK, BLOCK), f32),
            pltpu.VMEM((BLOCK, BLOCK), f32),
            pltpu.VMEM((BLOCK, BLOCK), f32),
            pltpu.VMEM((8 * covs, width), bf16),
            pltpu.VMEM((8 * covs, width), bf16),
            pltpu.VMEM((8 * covs, width), bf16),
        ],
        compiler_params=params,
        name="leaf",
    )(code, lane, scale, waves, signs, points, far)
    small = [pltpu.VMEM((rank, rank), f32), pltpu.VMEM((rank, rank), f32)]
    solved = pl.pallas_call(
        back_kernel,
        out_shape=jax.ShapeDtypeStruct((side, width), f32),
        in_specs=whole(2),
        out_specs=whole()[0],
        compiler_params=params,
        cost_estimate=pl.CostEstimate(flops=12 * side * width * width // 2, bytes_accessed=0, transcendentals=0),
        name="back",
    )(lower, aug)
    for height in range(1, levels):
        left = levels - height + 1
        other_first = partner_of(first, "leaf", height - 1)
        other_later = partner_of(later, "leaf", height - 1)
        other_first, solved = lax.optimization_barrier((other_first, solved))
        rest = side - height * rank
        coefficient, total = pl.pallas_call(
            height_kernel,
            out_shape=(jax.ShapeDtypeStruct((rest, rank), f32), jax.ShapeDtypeStruct((rest, rank), f32)),
            in_specs=whole(2),
            out_specs=tuple(whole(2)),
            scratch_shapes=small,
            compiler_params=params,
            name=f"height_{height}",
        )(first, other_first)
        outs = [jax.ShapeDtypeStruct((sizes[height], rank), f32)]
        if left > 2:
            outs.append(jax.ShapeDtypeStruct((sum(sizes[height + 1:]), rank), f32))
        found = pl.pallas_call(
            functools.partial(reduce_kernel, left),
            out_shape=tuple(outs),
            in_specs=whole(4),
            out_specs=tuple(whole(len(outs))),
            compiler_params=params,
            name=f"reduce_{height}",
        )(coefficient, total, later, other_later)
        first, later = found[0], found[-1]
        solved = pl.pallas_call(
            apply_kernel,
            out_shape=jax.ShapeDtypeStruct((rest, width), f32),
            in_specs=whole(2),
            out_specs=whole()[0],
            compiler_params=params,
            cost_estimate=pl.CostEstimate(flops=12 * rest * rank * width, bytes_accessed=0, transcendentals=0),
            name=f"apply_{height}",
        )(coefficient, solved)
    other = partner_of(first, "leaf", levels - 1)
    target_solve, probe_solves, terms, noise_grad = pl.pallas_call(
        final_kernel,
        out_shape=(
            jax.ShapeDtypeStruct((1, width), f32),
            jax.ShapeDtypeStruct((probes, width), f32),
            jax.ShapeDtypeStruct((1, width), f32),
            jax.ShapeDtypeStruct((1, width), f32),
        ),
        in_specs=whole(4),
        out_specs=tuple(whole(4)),
        scratch_shapes=small,
        compiler_params=params,
        name="final",
    )(first, other, solved, signs)
    probe_count = lax.axis_size("probe")
    for k in range(1, probe_count):
        noise_grad = noise_grad + lax.ppermute(terms, "probe", [(i, (i + k) % probe_count) for i in range(probe_count)])
    return (target_solve[0], probe_solves, noise_grad[0])


def solution(mesh):
    in_specs = (P(None, "leaf"), P("leaf"), P("leaf"), P(), P(), P(), P("leaf"), P("probe"))
    out_specs = (P("leaf"), P("probe", "leaf"), P("leaf"))
    return jax.shard_map(shards, mesh=mesh, in_specs=in_specs, out_specs=out_specs, check_vma=False)
```

```python
import functools
import math

import jax
import jax.numpy as jnp
from jax import lax
from jax.experimental import pallas as pl
from jax.experimental.pallas import tpu as pltpu
from jax.sharding import PartitionSpec as P

PROBES = 64
BLOCK = 256
SETTLED = 1.001
TAME = 256.0
SHARES = ((2, 2, 2, 2, 2), (2, 2, 2, 2, 2))

f32 = jnp.float32
bf16 = jnp.bfloat16
highest = lax.Precision.HIGHEST
hash_first = 747796405
hash_second = -1403630843
hash_third = -2073254261
VMEM_BYTES = 40 * 1024 * 1024


def partner_of(block, axis, apart):
    count = lax.axis_size(axis)
    return lax.ppermute(block, axis, [(i, i ^ (1 << apart)) for i in range(count)])


def halves(x):
    high = x.astype(bf16)
    return high, (x - high.astype(f32)).astype(bf16)


def thirds(x):
    high = x.astype(bf16)
    rest = x - high.astype(f32)
    middle = rest.astype(bf16)
    return high, middle, (rest - middle.astype(f32)).astype(bf16)


NN = (((1,), (0,)), ((), ()))
NT = (((1,), (1,)), ((), ()))
TN = (((0,), (0,)), ((), ()))


def dot_one(a, b, dims=NN):
    return lax.dot_general(a, b, dims, preferred_element_type=f32)


def dot_three(a, b, dims=NN):
    a_high, a_low = halves(a)
    b_high, b_low = halves(b)
    return dot_one(a_high, b_high, dims) + (dot_one(a_high, b_low, dims) + dot_one(a_low, b_high, dims))


def dot_full(a, b, dims=NN):
    return lax.dot_general(a, b, dims, precision=highest, preferred_element_type=f32)


def unit(size):
    rows = lax.broadcasted_iota(jnp.int32, (size, size), 0)
    columns = lax.broadcasted_iota(jnp.int32, (size, size), 1)
    return rows == columns


def gain(ratio):
    reach = (ratio - 1.0) / (ratio + 1.0)
    return 2.0 / (2.0 - reach * reach)


def tighter(ratio):
    return (ratio + 1.0) * (ratio + 1.0) / (4.0 * ratio)


def no_work(count):
    pass


def inverse(matrix, low, residual, approx, other_work=no_work, share=(0, 0, 0, 0, 0)):
    size = matrix.shape[0]
    same = unit(size)
    high = jnp.max(jnp.sum(jnp.abs(matrix), axis=0, keepdims=True)) * 1.0001
    low = jnp.minimum(low, high) * 0.9999
    scale = 2.0 / (low + high)
    ratio = high / low
    c = gain(ratio)
    first = jnp.where(same, 1.0, 0.0) - scale * matrix
    residual[...] = c * dot_three(first, first) - jnp.where(same, c - 1.0, 0.0)
    approx[...] = (c * scale) * (first + jnp.where(same, 1.0, 0.0))
    ratio = tighter(ratio)
    other_work(share[0])

    def more(ratio):
        return tighter(ratio) > SETTLED

    def double(ratio):
        c = gain(ratio)
        e = residual[...]
        x = approx[...]
        squared = dot_three(e, e)
        moved = dot_three(x, e)
        residual[...] = c * squared - jnp.where(same, c - 1.0, 0.0)
        approx[...] = c * (x + moved)
        return tighter(ratio)

    for step in (1, 2):
        ratio = double(ratio)
        other_work(share[step])
    ratio = lax.while_loop(more, double, ratio)
    x = approx[...]
    x = gain(ratio) * (x + dot_three(x, residual[...]))
    other_work(share[3])
    left = jnp.where(same, 1.0, 0.0) - dot_full(x, matrix)
    other_work(share[4])
    return x + dot_three(left, x)


def cosine(x):
    turns = jnp.floor(x * (1.0 / math.pi) + 0.5)
    r = x - turns * 3.140625
    r = r - turns * 9.67502593994140625e-4
    r = r - turns * 1.509957990978376e-7
    odd = jnp.bitwise_and(turns.astype(jnp.int32), 1)
    s = r * r
    value = 1.0 / 479001600.0
    for term in (-1.0 / 3628800.0, 1.0 / 40320.0, -1.0 / 720.0, 1.0 / 24.0, -0.5, 1.0):
        value = value * s + term
    return jnp.where(odd == 1, -value, value)


def logical_right(x, by):
    return lax.shift_right_logical(x, jnp.full_like(x, by))


def signs_of(seeds, positions):
    mixed = seeds * jnp.int32(hash_first) + positions * jnp.int32(hash_second)
    mixed = jnp.bitwise_xor(mixed, logical_right(mixed, 15))
    mixed = mixed * jnp.int32(hash_third)
    mixed = jnp.bitwise_xor(mixed, logical_right(mixed, 13))
    parity = jnp.bitwise_and(logical_right(mixed, 11), jnp.full_like(mixed, 1))
    return (2 * parity - 1).astype(f32)


def fetch(side, code_ref, lane_ref, ref, totals):
    chunks, lanes = code_ref.shape
    covs = totals[0][0].shape[0]
    size = chunks * (covs + 2)
    pieces = ref.shape[0] // size
    shape = (covs, lanes)
    codes = [jnp.broadcast_to(code_ref[k:k + 1, :], shape) for k in range(chunks)]
    places = [jnp.broadcast_to(lane_ref[k:k + 1, :], shape) for k in range(chunks)]
    rows = lax.broadcasted_iota(jnp.int32, (chunks, lanes), 0)

    def from_piece(piece, totals):
        coords, targets, noise = [list(t) for t in totals]
        number = (side * pieces + piece) * chunks
        start = pl.multiple_of(piece * size, 8)
        for c in range(chunks):
            source = ref[pl.ds(start + c * covs, covs), :]
            for k in range(chunks):
                coords[k] = jnp.where(codes[k] == number + c, jnp.take_along_axis(source, places[k], axis=1), coords[k])
        for at, found in ((chunks * covs, targets), (chunks * (covs + 1), noise)):
            source = ref[pl.ds(start + at, chunks), :]
            for k in range(chunks):
                found[k] = jnp.where(codes[k] == number + rows, jnp.take_along_axis(source, places[k], axis=1), found[k])
        return tuple(coords), tuple(targets), tuple(noise)

    return lax.fori_loop(0, pieces, from_piece, totals)


def near_kernel(code_ref, lane_ref, near_ref, point_ref):
    chunks, lanes = code_ref.shape
    totals = ((jnp.zeros((point_ref.shape[0] // (3 * chunks), lanes), f32),) * chunks,) * 3
    found = fetch(0, code_ref, lane_ref, near_ref, totals)
    point_ref[...] = jnp.concatenate([t for part in found for t in part], axis=0)


def points_of(code_ref, lane_ref, point_ref, far_ref):
    chunks = code_ref.shape[0]
    covs = point_ref.shape[0] // (3 * chunks)
    parts = [point_ref[k * covs:(k + 1) * covs, :] for k in range(3 * chunks)]
    totals = tuple(tuple(parts[k * chunks:(k + 1) * chunks]) for k in range(3))
    coords, targets, noise = fetch(1, code_ref, lane_ref, far_ref, totals)
    return (
        jnp.concatenate(coords, axis=1),
        jnp.concatenate([jnp.sum(t, axis=0, keepdims=True) for t in targets], axis=1),
        jnp.concatenate([jnp.sum(t, axis=0, keepdims=True) for t in noise], axis=1),
    )


def down(row, count):
    shape = (count, row.shape[1])
    same = lax.broadcasted_iota(jnp.int32, shape, 0) == lax.broadcasted_iota(jnp.int32, shape, 1)
    return jnp.sum(jnp.where(same, jnp.broadcast_to(row, shape), jnp.zeros(shape, row.dtype)), axis=1, keepdims=True)


def early_kernel(levels, nodes, place_ref, whole_ref, real_ref, code_ref, lane_ref, scale_ref, wave_ref, sign_ref):
    chunks, lanes = code_ref.shape
    covs = scale_ref.shape[0]
    leaf = place_ref[0]
    half = 1 << (levels - 1)
    order = whole_ref[:chunks, :]
    owner = jnp.right_shift(order, (chunks * lanes).bit_length() - 1)
    chunk = jnp.bitwise_and(jnp.right_shift(order, lanes.bit_length() - 1), chunks - 1)
    across = jnp.bitwise_and(jnp.bitwise_xor(owner, leaf), 1)
    turn = jnp.bitwise_and(jnp.right_shift(jnp.bitwise_xor(leaf, across) - owner, 1), half - 1)
    code_ref[...] = (across * half + turn) * chunks + chunk
    lane_ref[...] = jnp.bitwise_and(order, lanes - 1)
    scale_ref[...] = jnp.broadcast_to(down(real_ref[nodes * (covs + 1):nodes * (covs + 1) + 1, :], covs), scale_ref.shape)
    rank = wave_ref.shape[2]
    at_row = lax.broadcasted_iota(jnp.int32, (8, rank), 0)
    for level in range(levels):
        node = jnp.right_shift((1 << levels) + leaf, level + 1) - 1
        fh, fm, fl = [p.astype(f32) for p in thirds(real_ref[pl.ds(pl.multiple_of(node * covs, covs), covs), :])]
        ph, pm, p_low = [p.astype(f32) for p in thirds(real_ref[pl.ds(nodes * covs + node, 1), :])]
        phases = jnp.where(at_row == 0, ph, jnp.where(at_row == 1, pm, jnp.where(at_row == 2, p_low, 0.0)))
        wave_ref[level] = jnp.concatenate([fh, fh, fm, fm, fh, fl, phases, jnp.zeros_like(phases)], axis=0)
    probes, width = sign_ref.shape
    positions = leaf * width + lax.broadcasted_iota(jnp.int32, (probes, width), 1)
    sign_ref[...] = signs_of(down(whole_ref[chunks:chunks + 1, :], probes), positions)


def leaf_kernel(levels, code_ref, lane_ref, scale_ref, wave_ref, sign_ref, point_ref, far_ref,
                lower_ref, aug_ref, first_ref, rest_ref, matrix, inverses, residual, approx,
                left_points, right_points, basis_points):
    probes, width = sign_ref.shape
    rank = wave_ref.shape[2]
    covs = scale_ref.shape[0]
    blocks = width // BLOCK
    top = width + levels * rank
    coords, targets, noise = points_of(code_ref, lane_ref, point_ref, far_ref)
    u = coords / scale_ref[:, :1]
    s = -0.5 * jnp.sum(u * u, axis=0, keepdims=True)
    rows = matrix.shape[0]
    h, m, l = [p.astype(f32) for p in thirds(u)]
    row = lax.broadcasted_iota(jnp.int32, (8, width), 0)
    ones = jnp.where(row < 3, 1.0, 0.0)
    same = unit(BLOCK)
    spans = [slice(k * BLOCK, (k + 1) * BLOCK) for k in range(blocks)]
    side_ranges = [(start, min(start + BLOCK, rows)) for start in range(width, rows, BLOCK)]
    leaf_ranges = [(k * BLOCK, (k + 1) * BLOCK) for k in range(blocks)]
    s_parts = [p.astype(f32) for p in thirds(s)]
    s_rows = jnp.where(row == 0, s_parts[0], jnp.where(row == 1, s_parts[1], jnp.where(row == 2, s_parts[2], 0.0)))
    left_points[...] = jnp.concatenate([h, h, m, m, h, l, s_rows, ones], axis=0).astype(bf16)
    right_points[...] = jnp.concatenate([h, m, h, m, l, h, ones, s_rows], axis=0).astype(bf16)
    basis_points[...] = jnp.concatenate([h, m, h, m, l, h, ones, ones], axis=0).astype(bf16)

    def build(i, j):
        part = jnp.exp(dot_one(left_points[:, spans[i]], right_points[:, spans[j]], TN))
        if i == j:
            part = part + jnp.where(same, noise[:, spans[i]], 0.0)
        matrix[spans[i], spans[j]] = part

    def basis(level):
        angle = dot_one(wave_ref[level].astype(bf16), basis_points[...], TN)
        matrix[width + level * rank:width + (level + 1) * rank, :] = math.sqrt(2.0 / rank) * cosine(angle)

    def right_sides():
        matrix[top:top + probes, :] = sign_ref[...]
        matrix[top + probes:, :] = jnp.concatenate([targets, jnp.zeros((rows - top - probes - 1, width), f32)], axis=0)

    def weights_at(rows_of, k):
        start, end = rows_of
        if start < width:
            return lower_ref.at[start - BLOCK:end - BLOCK, spans[k]]
        return aug_ref.at[start - width:end - width, spans[k]]

    def all_steps(dot):
        def weigh(rows_of, k):
            weights_at(rows_of, k)[...] = dot(matrix[rows_of[0]:rows_of[1], spans[k]], inverses[k % 2])

        def update(rows_of, j, k):
            here = slice(*rows_of)
            matrix[here, spans[j]] = matrix[here, spans[j]] - dot(weights_at(rows_of, k)[...], matrix[spans[j], spans[k]], NT)

        def add_up(level, k):
            many = min(2, levels - level)
            start = level * rank
            columns = matrix[width + start:width + start + many * rank, spans[k]]
            part = dot_three(aug_ref[start:, spans[k]], columns, NT)
            for next_to in range(many):
                column = level + next_to
                at = sum(rows - width - before * rank for before in range(1, column))
                count = rows - width - column * rank
                piece = part[next_to * rank:, next_to * rank:(next_to + 1) * rank]
                kept = (rest_ref if column else first_ref).at[at:at + count, :]
                kept[...] = piece if k == 0 else kept[...] + piece

        tasks, done, queue = {}, set(), []

        def add(key, call, after=()):
            tasks[key] = (call, after)
            queue.append(key)

        def run(key):
            if key not in done:
                done.add(key)
                call, after = tasks[key]
                for other in after:
                    run(other)
                call()

        def other_work(count):
            while count and queue:
                key = queue.pop(0)
                if key not in done:
                    run(key)
                    count -= 1

        def ready(rows_of, j, k):
            if rows_of[0] < width:
                first = [("build", rows_of[0] // BLOCK, j)]
            else:
                first = [("basis", level) for level in range(levels)] + [("right",)]
            return first + [("update", rows_of, j, before) for before in range(k)]

        for j in range(blocks):
            done.add(("build", j, j))
            for i in range(j + 1, blocks):
                add(("build", i, j), functools.partial(build, i, j))
            if j == 0:
                for level in range(levels):
                    add(("basis", level), functools.partial(basis, level))
                add(("right",), right_sides)
        for k in range(blocks):
            for key in ready(leaf_ranges[k], k, k):
                run(key)
            found = inverse(matrix[spans[k], spans[k]], jnp.min(noise[:, spans[k]]), residual, approx, other_work, SHARES[min(k, 1)])
            if k > 1:
                for key in tasks:
                    if key[0] == "weigh" and key[2] == k - 2:
                        run(key)
            inverses[k % 2] = found
            ranges = leaf_ranges[k + 1:] + side_ranges
            for rows_of in ranges:
                add(("weigh", rows_of, k), functools.partial(weigh, rows_of, k), ready(rows_of, k, k))
            for j in range(k + 1, blocks):
                for rows_of in leaf_ranges[j:] + side_ranges:
                    add(("update", rows_of, j, k), functools.partial(update, rows_of, j, k),
                        ready(rows_of, j, 0) + ready(leaf_ranges[j], k, k) + [("weigh", rows_of, k)])
            for level in range(0, levels, 2):
                add(("sum", level, k), functools.partial(add_up, level, k),
                    [("weigh", rows_of, k) for rows_of in side_ranges]
                    + [key for rows_of in side_ranges for key in ready(rows_of, k, k)])
        other_work(len(queue))

    def all_full():
        side = rows - width
        chunk = max(c for c in range(8, BLOCK + 1, 8) if side % c == 0)

        def span_of(k, size=BLOCK, start=0):
            return pl.ds(pl.multiple_of(start + k * size, 8 if size < BLOCK else BLOCK), size)

        def rebuild(i, carry):
            part = jnp.exp(dot_one(left_points[:, span_of(i)], right_points[...], TN))
            row = i * BLOCK + lax.broadcasted_iota(jnp.int32, (BLOCK, width), 0)
            matrix[span_of(i), :] = part + jnp.where(row == lax.broadcasted_iota(jnp.int32, (BLOCK, width), 1), noise, 0.0)
            return carry

        def wave(level, carry):
            angle = dot_one(wave_ref[level].astype(bf16), basis_points[...], TN)
            matrix[pl.ds(pl.multiple_of(width + level * rank, rank), rank), :] = math.sqrt(2.0 / rank) * cosine(angle)
            return carry

        def step(k, carry):
            here = span_of(k)
            inverses[0] = inverse(matrix[here, here], jnp.min(noise), residual, approx)

            def weigh_leaf(r, carry):
                lower_ref[span_of(r - 1), here] = dot_full(matrix[span_of(r), here], inverses[0])
                return carry

            def weigh_side(r, carry):
                aug_ref[span_of(r, chunk), here] = dot_full(matrix[span_of(r, chunk, width), here], inverses[0])
                return carry

            def column(j, carry):
                there = span_of(j)

                def update_leaf(r, carry):
                    matrix[span_of(r), there] -= dot_full(lower_ref[span_of(r - 1), here], matrix[there, here], NT)
                    return carry

                def update_side(r, carry):
                    at = span_of(r, chunk, width)
                    matrix[at, there] -= dot_full(aug_ref[span_of(r, chunk), here], matrix[there, here], NT)
                    return carry

                lax.fori_loop(j, blocks, update_leaf, 0)
                return lax.fori_loop(0, side // chunk, update_side, carry)

            lax.fori_loop(k + 1, blocks, weigh_leaf, 0)
            lax.fori_loop(0, side // chunk, weigh_side, 0)
            return lax.fori_loop(k + 1, blocks, column, carry)

        lax.fori_loop(0, blocks, rebuild, 0)
        lax.fori_loop(0, levels, wave, 0)
        right_sides()
        lax.fori_loop(0, blocks, step, 0)
        for level in range(levels):
            at = sum(side - before * rank for before in range(1, level))
            kept = rest_ref if level else first_ref

            def add_rows(r, carry):
                kept[span_of(r, 8, at), :] = dot_full(
                    aug_ref[span_of(r, 8, level * rank), :], matrix[width + level * rank:width + (level + 1) * rank, :], NT)
                return carry

            lax.fori_loop(0, (side - level * rank) // 8, add_rows, 0)

    total = jnp.zeros((), f32)
    for k in range(blocks):
        build(k, k)
        total = total + jnp.max(jnp.sum(matrix[spans[k], spans[k]], axis=0, keepdims=True))
    tame = total <= TAME * jnp.min(noise)

    all_steps(dot_three)

    @pl.when(jnp.logical_not(tame))
    def _():
        all_full()


def eliminate(own, other, rank, residual, approx):
    total = own + other
    capacitance = total[:rank] + jnp.where(unit(rank), 1.0, 0.0)
    return total, dot_full(total[rank:], inverse(capacitance, jnp.float32(1.0), residual, approx))


def height_kernel(own_ref, other_ref, coefficient_ref, total_ref, residual, approx):
    total, coefficients = eliminate(own_ref[...], other_ref[...], own_ref.shape[1], residual, approx)
    coefficient_ref[...] = coefficients
    total_ref[...] = total[own_ref.shape[1]:]


def reduce_kernel(left, coefficient_ref, total_ref, own_ref, other_ref, *out_refs):
    rank = own_ref.shape[1]
    at = to = 0
    for level in range(1, left):
        start = (level - 1) * rank
        size = coefficient_ref.shape[0] - start
        value = own_ref[at:at + size, :] + other_ref[at:at + size, :] - dot_full(
            coefficient_ref[start:, :], total_ref[start:start + rank, :], NT)
        if level == 1:
            out_refs[0][...] = value
        else:
            out_refs[1][to:to + size, :] = value
            to += size
        at += size


def back_kernel(lower_ref, aug_ref, solved_ref):
    width = aug_ref.shape[1]
    spans = [slice(k * BLOCK, (k + 1) * BLOCK) for k in range(width // BLOCK)]
    for k in range(len(spans) - 1, -1, -1):
        value = aug_ref[:, spans[k]]
        for j in range(k + 1, len(spans)):
            value = value - dot_full(solved_ref[:, spans[j]], lower_ref[(j - 1) * BLOCK:j * BLOCK, spans[k]])
        solved_ref[:, spans[k]] = value


def apply_kernel(coefficient_ref, solved_ref, rest_ref):
    rank = coefficient_ref.shape[1]
    rest_ref[...] = solved_ref[rank:, :] - dot_full(coefficient_ref[...], solved_ref[:rank, :])


def final_kernel(own_ref, other_ref, solved_ref, sign_ref, target_ref, solve_ref, terms_ref, all_ref, residual, approx):
    rank = own_ref.shape[1]
    probes = sign_ref.shape[0]
    _, last = eliminate(own_ref[...], other_ref[...], rank, residual, approx)
    solved = solved_ref[rank:, :] - dot_full(last, solved_ref[:rank, :])
    solve_ref[...] = solved[:probes]
    target = solved[probes:probes + 1]
    target_ref[...] = target
    terms = (-0.5 / PROBES) * jnp.sum(sign_ref[...] * solved[:probes], axis=0, keepdims=True)
    terms_ref[...] = terms
    all_ref[...] = 0.5 * target * target + terms


def whole(count=1):
    return [pl.BlockSpec(memory_space=pltpu.VMEM)] * count


def scalars():
    return pl.BlockSpec(memory_space=pltpu.SMEM)


def shards(covariates, targets, noise_var, lengths, frequencies, phases, tree_order, probe_seeds):
    leaf_count = lax.axis_size("leaf")
    leaf_index = lax.axis_index("leaf")
    width = tree_order.shape[0]
    rank = phases.shape[1]
    probes = probe_seeds.shape[0]
    levels = leaf_count.bit_length() - 1
    tail = -(-(probes + 1) // 8) * 8
    lanes = 128
    chunks = width // lanes
    covs = covariates.shape[0]
    piece = jnp.concatenate(
        [
            covariates.reshape(covs, chunks, lanes).transpose(1, 0, 2).reshape(chunks * covs, lanes),
            targets.reshape(chunks, lanes),
            noise_var.reshape(chunks, lanes),
        ],
        axis=0,
    )
    piece = lax.optimization_barrier(piece)
    pieces = [piece]
    for k in range(2, leaf_count, 2):
        pieces.append(lax.ppermute(piece, "leaf", [(i, (i + k) % leaf_count) for i in range(leaf_count)]))
    near = jnp.concatenate(pieces, axis=0)
    place = leaf_index[None].astype(jnp.int32)
    sizes = [(levels - level) * rank + tail for level in range(levels)]
    params = pltpu.CompilerParams(vmem_limit_bytes=VMEM_BYTES)
    nodes = phases.shape[0]
    integers = jnp.concatenate([tree_order.reshape(chunks, lanes), jnp.pad(probe_seeds, (0, lanes - probes))[None]], axis=0)
    reals = jnp.concatenate([frequencies.reshape(nodes * covs, rank), phases, jnp.pad(lengths, (0, rank - covs))[None]], axis=0)
    code, lane, scale, waves, signs = pl.pallas_call(
        functools.partial(early_kernel, levels, nodes),
        out_shape=(
            jax.ShapeDtypeStruct((chunks, lanes), jnp.int32),
            jax.ShapeDtypeStruct((chunks, lanes), jnp.int32),
            jax.ShapeDtypeStruct((covs, lanes), f32),
            jax.ShapeDtypeStruct((levels, 8 * covs, rank), f32),
            jax.ShapeDtypeStruct((probes, width), f32),
        ),
        in_specs=[scalars()] + whole(2),
        out_specs=tuple(whole(5)),
        compiler_params=params,
        name="early",
    )(place, integers, reals)
    near, code, lane, scale, waves, signs = lax.optimization_barrier((near, code, lane, scale, waves, signs))
    far = partner_of(near, "leaf", 0)
    points = pl.pallas_call(
        near_kernel,
        out_shape=jax.ShapeDtypeStruct((3 * chunks * covs, lanes), f32),
        in_specs=whole(3),
        out_specs=whole()[0],
        compiler_params=params,
        cost_estimate=pl.CostEstimate(flops=10**9, bytes_accessed=0, transcendentals=0),
        name="near",
    )(code, lane, near)
    far, points = lax.optimization_barrier((far, points))
    side = levels * rank + tail
    lower, aug, first, later = pl.pallas_call(
        functools.partial(leaf_kernel, levels),
        out_shape=(
            jax.ShapeDtypeStruct((width - BLOCK, width - BLOCK), f32),
            jax.ShapeDtypeStruct((side, width), f32),
            jax.ShapeDtypeStruct((sizes[0], rank), f32),
            jax.ShapeDtypeStruct((sum(sizes[1:]), rank), f32),
        ),
        in_specs=whole(7),
        out_specs=tuple(whole(4)),
        scratch_shapes=[
            pltpu.VMEM((width + side, width), f32),
            pltpu.VMEM((2, BLOCK, BLOCK), f32),
            pltpu.VMEM((BLOCK, BLOCK), f32),
            pltpu.VMEM((BLOCK, BLOCK), f32),
            pltpu.VMEM((8 * covs, width), bf16),
            pltpu.VMEM((8 * covs, width), bf16),
            pltpu.VMEM((8 * covs, width), bf16),
        ],
        compiler_params=params,
        name="leaf",
    )(code, lane, scale, waves, signs, points, far)
    small = [pltpu.VMEM((rank, rank), f32), pltpu.VMEM((rank, rank), f32)]
    solved = pl.pallas_call(
        back_kernel,
        out_shape=jax.ShapeDtypeStruct((side, width), f32),
        in_specs=whole(2),
        out_specs=whole()[0],
        compiler_params=params,
        cost_estimate=pl.CostEstimate(flops=12 * side * width * width // 2, bytes_accessed=0, transcendentals=0),
        name="back",
    )(lower, aug)
    for height in range(1, levels):
        left = levels - height + 1
        other_first = partner_of(first, "leaf", height - 1)
        other_later = partner_of(later, "leaf", height - 1)
        other_first, solved = lax.optimization_barrier((other_first, solved))
        rest = side - height * rank
        coefficient, total = pl.pallas_call(
            height_kernel,
            out_shape=(jax.ShapeDtypeStruct((rest, rank), f32), jax.ShapeDtypeStruct((rest, rank), f32)),
            in_specs=whole(2),
            out_specs=tuple(whole(2)),
            scratch_shapes=small,
            compiler_params=params,
            name=f"height_{height}",
        )(first, other_first)
        outs = [jax.ShapeDtypeStruct((sizes[height], rank), f32)]
        if left > 2:
            outs.append(jax.ShapeDtypeStruct((sum(sizes[height + 1:]), rank), f32))
        found = pl.pallas_call(
            functools.partial(reduce_kernel, left),
            out_shape=tuple(outs),
            in_specs=whole(4),
            out_specs=tuple(whole(len(outs))),
            compiler_params=params,
            name=f"reduce_{height}",
        )(coefficient, total, later, other_later)
        first, later = found[0], found[-1]
        solved = pl.pallas_call(
            apply_kernel,
            out_shape=jax.ShapeDtypeStruct((rest, width), f32),
            in_specs=whole(2),
            out_specs=whole()[0],
            compiler_params=params,
            cost_estimate=pl.CostEstimate(flops=12 * rest * rank * width, bytes_accessed=0, transcendentals=0),
            name=f"apply_{height}",
        )(coefficient, solved)
    other = partner_of(first, "leaf", levels - 1)
    target_solve, probe_solves, terms, noise_grad = pl.pallas_call(
        final_kernel,
        out_shape=(
            jax.ShapeDtypeStruct((1, width), f32),
            jax.ShapeDtypeStruct((probes, width), f32),
            jax.ShapeDtypeStruct((1, width), f32),
            jax.ShapeDtypeStruct((1, width), f32),
        ),
        in_specs=whole(4),
        out_specs=tuple(whole(4)),
        scratch_shapes=small,
        compiler_params=params,
        name="final",
    )(first, other, solved, signs)
    probe_count = lax.axis_size("probe")
    for k in range(1, probe_count):
        noise_grad = noise_grad + lax.ppermute(terms, "probe", [(i, i ^ k) for i in range(probe_count)])
    return (target_solve[0], probe_solves, noise_grad[0])


def solution(mesh):
    in_specs = (P(None, "leaf"), P("leaf"), P("leaf"), P(), P(), P(), P("leaf"), P("probe"))
    out_specs = (P("leaf"), P("probe", "leaf"), P("leaf"))
    return jax.shard_map(shards, mesh=mesh, in_specs=in_specs, out_specs=out_specs, check_vma=False)
```

```python
import functools
import math

import jax
import jax.numpy as jnp
from jax import lax
from jax.experimental import pallas as pl
from jax.experimental.pallas import tpu as pltpu
from jax.sharding import PartitionSpec as P

PROBES = 64
BLOCK = 256
SETTLED = 1.001
TAME = 256.0
SHARES = ((2, 2, 2, 2, 2), (2, 2, 2, 2, 2))

f32 = jnp.float32
bf16 = jnp.bfloat16
highest = lax.Precision.HIGHEST
hash_first = 747796405
hash_second = -1403630843
hash_third = -2073254261
VMEM_BYTES = 40 * 1024 * 1024


def partner_of(block, axis, apart):
    count = lax.axis_size(axis)
    return lax.ppermute(block, axis, [(i, i ^ (1 << apart)) for i in range(count)])


def halves(x):
    high = x.astype(bf16)
    return high, (x - high.astype(f32)).astype(bf16)


def thirds(x):
    high = x.astype(bf16)
    rest = x - high.astype(f32)
    middle = rest.astype(bf16)
    return high, middle, (rest - middle.astype(f32)).astype(bf16)


NN = (((1,), (0,)), ((), ()))
NT = (((1,), (1,)), ((), ()))
TN = (((0,), (0,)), ((), ()))


def dot_one(a, b, dims=NN):
    return lax.dot_general(a, b, dims, preferred_element_type=f32)


def dot_three(a, b, dims=NN):
    a_high, a_low = halves(a)
    b_high, b_low = halves(b)
    return dot_one(a_high, b_high, dims) + (dot_one(a_high, b_low, dims) + dot_one(a_low, b_high, dims))


def dot_full(a, b, dims=NN):
    return lax.dot_general(a, b, dims, precision=highest, preferred_element_type=f32)


def unit(size):
    rows = lax.broadcasted_iota(jnp.int32, (size, size), 0)
    columns = lax.broadcasted_iota(jnp.int32, (size, size), 1)
    return rows == columns


def gain(ratio):
    reach = (ratio - 1.0) / (ratio + 1.0)
    return 2.0 / (2.0 - reach * reach)


def tighter(ratio):
    return (ratio + 1.0) * (ratio + 1.0) / (4.0 * ratio)


def no_work(count):
    pass


def inverse(matrix, low, residual, approx, other_work=no_work, share=(0, 0, 0, 0, 0)):
    size = matrix.shape[0]
    same = unit(size)
    high = jnp.max(jnp.sum(jnp.abs(matrix), axis=0, keepdims=True)) * 1.0001
    low = jnp.minimum(low, high) * 0.9999
    scale = 2.0 / (low + high)
    ratio = high / low
    c = gain(ratio)
    first = jnp.where(same, 1.0, 0.0) - scale * matrix
    residual[...] = c * dot_three(first, first) - jnp.where(same, c - 1.0, 0.0)
    approx[...] = (c * scale) * (first + jnp.where(same, 1.0, 0.0))
    ratio = tighter(ratio)
    other_work(share[0])

    def more(ratio):
        return tighter(ratio) > SETTLED

    def double(ratio):
        c = gain(ratio)
        e = residual[...]
        x = approx[...]
        squared = dot_three(e, e)
        moved = dot_three(x, e)
        residual[...] = c * squared - jnp.where(same, c - 1.0, 0.0)
        approx[...] = c * (x + moved)
        return tighter(ratio)

    for step in (1, 2):
        ratio = double(ratio)
        other_work(share[step])
    ratio = lax.while_loop(more, double, ratio)
    x = approx[...]
    x = gain(ratio) * (x + dot_three(x, residual[...]))
    other_work(share[3])
    left = jnp.where(same, 1.0, 0.0) - dot_full(x, matrix)
    other_work(share[4])
    return x + dot_three(left, x)


def cosine(x):
    turns = jnp.floor(x * (1.0 / math.pi) + 0.5)
    r = x - turns * 3.140625
    r = r - turns * 9.67502593994140625e-4
    r = r - turns * 1.509957990978376e-7
    odd = jnp.bitwise_and(turns.astype(jnp.int32), 1)
    s = r * r
    value = 1.0 / 479001600.0
    for term in (-1.0 / 3628800.0, 1.0 / 40320.0, -1.0 / 720.0, 1.0 / 24.0, -0.5, 1.0):
        value = value * s + term
    return jnp.where(odd == 1, -value, value)


def logical_right(x, by):
    return lax.shift_right_logical(x, jnp.full_like(x, by))


def signs_of(seeds, positions):
    mixed = seeds * jnp.int32(hash_first) + positions * jnp.int32(hash_second)
    mixed = jnp.bitwise_xor(mixed, logical_right(mixed, 15))
    mixed = mixed * jnp.int32(hash_third)
    mixed = jnp.bitwise_xor(mixed, logical_right(mixed, 13))
    parity = jnp.bitwise_and(logical_right(mixed, 11), jnp.full_like(mixed, 1))
    return (2 * parity - 1).astype(f32)


def fetch(side, code_ref, lane_ref, ref, totals):
    chunks, lanes = code_ref.shape
    covs = totals[0][0].shape[0]
    size = chunks * (covs + 2)
    pieces = ref.shape[0] // size
    shape = (covs, lanes)
    codes = [jnp.broadcast_to(code_ref[k:k + 1, :], shape) for k in range(chunks)]
    places = [jnp.broadcast_to(lane_ref[k:k + 1, :], shape) for k in range(chunks)]
    rows = lax.broadcasted_iota(jnp.int32, (chunks, lanes), 0)

    def from_piece(piece, totals):
        coords, targets, noise = [list(t) for t in totals]
        number = (side * pieces + piece) * chunks
        start = pl.multiple_of(piece * size, 8)
        for c in range(chunks):
            source = ref[pl.ds(start + c * covs, covs), :]
            for k in range(chunks):
                coords[k] = jnp.where(codes[k] == number + c, jnp.take_along_axis(source, places[k], axis=1), coords[k])
        for at, found in ((chunks * covs, targets), (chunks * (covs + 1), noise)):
            source = ref[pl.ds(start + at, chunks), :]
            for k in range(chunks):
                found[k] = jnp.where(codes[k] == number + rows, jnp.take_along_axis(source, places[k], axis=1), found[k])
        return tuple(coords), tuple(targets), tuple(noise)

    return lax.fori_loop(0, pieces, from_piece, totals)


def near_kernel(code_ref, lane_ref, near_ref, point_ref):
    chunks, lanes = code_ref.shape
    totals = ((jnp.zeros((point_ref.shape[0] // (3 * chunks), lanes), f32),) * chunks,) * 3
    found = fetch(0, code_ref, lane_ref, near_ref, totals)
    point_ref[...] = jnp.concatenate([t for part in found for t in part], axis=0)


def points_of(code_ref, lane_ref, point_ref, far_ref):
    chunks = code_ref.shape[0]
    covs = point_ref.shape[0] // (3 * chunks)
    parts = [point_ref[k * covs:(k + 1) * covs, :] for k in range(3 * chunks)]
    totals = tuple(tuple(parts[k * chunks:(k + 1) * chunks]) for k in range(3))
    coords, targets, noise = fetch(1, code_ref, lane_ref, far_ref, totals)
    return (
        jnp.concatenate(coords, axis=1),
        jnp.concatenate([jnp.sum(t, axis=0, keepdims=True) for t in targets], axis=1),
        jnp.concatenate([jnp.sum(t, axis=0, keepdims=True) for t in noise], axis=1),
    )


def down(row, count):
    shape = (count, row.shape[1])
    same = lax.broadcasted_iota(jnp.int32, shape, 0) == lax.broadcasted_iota(jnp.int32, shape, 1)
    return jnp.sum(jnp.where(same, jnp.broadcast_to(row, shape), jnp.zeros(shape, row.dtype)), axis=1, keepdims=True)


def early_kernel(levels, nodes, place_ref, whole_ref, real_ref, code_ref, lane_ref, scale_ref, wave_ref, sign_ref):
    chunks, lanes = code_ref.shape
    covs = scale_ref.shape[0]
    leaf = place_ref[0]
    half = 1 << (levels - 1)
    order = whole_ref[:chunks, :]
    owner = jnp.right_shift(order, (chunks * lanes).bit_length() - 1)
    chunk = jnp.bitwise_and(jnp.right_shift(order, lanes.bit_length() - 1), chunks - 1)
    across = jnp.bitwise_and(jnp.bitwise_xor(owner, leaf), 1)
    turn = jnp.bitwise_and(jnp.right_shift(jnp.bitwise_xor(leaf, owner), 1), half - 1)
    code_ref[...] = (across * half + turn) * chunks + chunk
    lane_ref[...] = jnp.bitwise_and(order, lanes - 1)
    scale_ref[...] = jnp.broadcast_to(down(real_ref[nodes * (covs + 1):nodes * (covs + 1) + 1, :], covs), scale_ref.shape)
    rank = wave_ref.shape[2]
    at_row = lax.broadcasted_iota(jnp.int32, (8, rank), 0)
    for level in range(levels):
        node = jnp.right_shift((1 << levels) + leaf, level + 1) - 1
        fh, fm, fl = [p.astype(f32) for p in thirds(real_ref[pl.ds(pl.multiple_of(node * covs, covs), covs), :])]
        ph, pm, p_low = [p.astype(f32) for p in thirds(real_ref[pl.ds(nodes * covs + node, 1), :])]
        phases = jnp.where(at_row == 0, ph, jnp.where(at_row == 1, pm, jnp.where(at_row == 2, p_low, 0.0)))
        wave_ref[level] = jnp.concatenate([fh, fh, fm, fm, fh, fl, phases, jnp.zeros_like(phases)], axis=0)
    probes, width = sign_ref.shape
    positions = leaf * width + lax.broadcasted_iota(jnp.int32, (probes, width), 1)
    sign_ref[...] = signs_of(down(whole_ref[chunks:chunks + 1, :], probes), positions)


def leaf_kernel(levels, code_ref, lane_ref, scale_ref, wave_ref, sign_ref, point_ref, far_ref,
                lower_ref, aug_ref, first_ref, rest_ref, matrix, inverses, residual, approx,
                left_points, right_points, basis_points):
    probes, width = sign_ref.shape
    rank = wave_ref.shape[2]
    covs = scale_ref.shape[0]
    blocks = width // BLOCK
    top = width + levels * rank
    coords, targets, noise = points_of(code_ref, lane_ref, point_ref, far_ref)
    u = coords / scale_ref[:, :1]
    s = -0.5 * jnp.sum(u * u, axis=0, keepdims=True)
    rows = matrix.shape[0]
    h, m, l = [p.astype(f32) for p in thirds(u)]
    row = lax.broadcasted_iota(jnp.int32, (8, width), 0)
    ones = jnp.where(row < 3, 1.0, 0.0)
    same = unit(BLOCK)
    spans = [slice(k * BLOCK, (k + 1) * BLOCK) for k in range(blocks)]
    side_ranges = [(start, min(start + BLOCK, rows)) for start in range(width, rows, BLOCK)]
    leaf_ranges = [(k * BLOCK, (k + 1) * BLOCK) for k in range(blocks)]
    s_parts = [p.astype(f32) for p in thirds(s)]
    s_rows = jnp.where(row == 0, s_parts[0], jnp.where(row == 1, s_parts[1], jnp.where(row == 2, s_parts[2], 0.0)))
    left_points[...] = jnp.concatenate([h, h, m, m, h, l, s_rows, ones], axis=0).astype(bf16)
    right_points[...] = jnp.concatenate([h, m, h, m, l, h, ones, s_rows], axis=0).astype(bf16)
    basis_points[...] = jnp.concatenate([h, m, h, m, l, h, ones, ones], axis=0).astype(bf16)

    def build(i, j):
        part = jnp.exp(dot_one(left_points[:, spans[i]], right_points[:, spans[j]], TN))
        if i == j:
            part = part + jnp.where(same, noise[:, spans[i]], 0.0)
        matrix[spans[i], spans[j]] = part

    def basis(level):
        angle = dot_one(wave_ref[level].astype(bf16), basis_points[...], TN)
        matrix[width + level * rank:width + (level + 1) * rank, :] = math.sqrt(2.0 / rank) * cosine(angle)

    def right_sides():
        matrix[top:top + probes, :] = sign_ref[...]
        matrix[top + probes:, :] = jnp.concatenate([targets, jnp.zeros((rows - top - probes - 1, width), f32)], axis=0)

    def weights_at(rows_of, k):
        start, end = rows_of
        if start < width:
            return lower_ref.at[start - BLOCK:end - BLOCK, spans[k]]
        return aug_ref.at[start - width:end - width, spans[k]]

    def all_steps(dot):
        def weigh(rows_of, k):
            weights_at(rows_of, k)[...] = dot(matrix[rows_of[0]:rows_of[1], spans[k]], inverses[k % 2])

        def update(rows_of, j, k):
            here = slice(*rows_of)
            matrix[here, spans[j]] = matrix[here, spans[j]] - dot(weights_at(rows_of, k)[...], matrix[spans[j], spans[k]], NT)

        def add_up(level, k):
            many = min(2, levels - level)
            start = level * rank
            columns = matrix[width + start:width + start + many * rank, spans[k]]
            part = dot_three(aug_ref[start:, spans[k]], columns, NT)
            for next_to in range(many):
                column = level + next_to
                at = sum(rows - width - before * rank for before in range(1, column))
                count = rows - width - column * rank
                piece = part[next_to * rank:, next_to * rank:(next_to + 1) * rank]
                kept = (rest_ref if column else first_ref).at[at:at + count, :]
                kept[...] = piece if k == 0 else kept[...] + piece

        tasks, done, queue = {}, set(), []

        def add(key, call, after=()):
            tasks[key] = (call, after)
            queue.append(key)

        def run(key):
            if key not in done:
                done.add(key)
                call, after = tasks[key]
                for other in after:
                    run(other)
                call()

        def other_work(count):
            while count and queue:
                key = queue.pop(0)
                if key not in done:
                    run(key)
                    count -= 1

        def ready(rows_of, j, k):
            if rows_of[0] < width:
                first = [("build", rows_of[0] // BLOCK, j)]
            else:
                first = [("basis", level) for level in range(levels)] + [("right",)]
            return first + [("update", rows_of, j, before) for before in range(k)]

        for j in range(blocks):
            done.add(("build", j, j))
            for i in range(j + 1, blocks):
                add(("build", i, j), functools.partial(build, i, j))
            if j == 0:
                for level in range(levels):
                    add(("basis", level), functools.partial(basis, level))
                add(("right",), right_sides)
        for k in range(blocks):
            for key in ready(leaf_ranges[k], k, k):
                run(key)
            found = inverse(matrix[spans[k], spans[k]], jnp.min(noise[:, spans[k]]), residual, approx, other_work, SHARES[min(k, 1)])
            if k > 1:
                for key in tasks:
                    if key[0] == "weigh" and key[2] == k - 2:
                        run(key)
            inverses[k % 2] = found
            ranges = leaf_ranges[k + 1:] + side_ranges
            for rows_of in ranges:
                add(("weigh", rows_of, k), functools.partial(weigh, rows_of, k), ready(rows_of, k, k))
            for j in range(k + 1, blocks):
                for rows_of in leaf_ranges[j:] + side_ranges:
                    add(("update", rows_of, j, k), functools.partial(update, rows_of, j, k),
                        ready(rows_of, j, 0) + ready(leaf_ranges[j], k, k) + [("weigh", rows_of, k)])
            for level in range(0, levels, 2):
                add(("sum", level, k), functools.partial(add_up, level, k),
                    [("weigh", rows_of, k) for rows_of in side_ranges]
                    + [key for rows_of in side_ranges for key in ready(rows_of, k, k)])
        other_work(len(queue))

    def all_full():
        side = rows - width
        chunk = max(c for c in range(8, BLOCK + 1, 8) if side % c == 0)

        def span_of(k, size=BLOCK, start=0):
            return pl.ds(pl.multiple_of(start + k * size, 8 if size < BLOCK else BLOCK), size)

        def rebuild(i, carry):
            part = jnp.exp(dot_one(left_points[:, span_of(i)], right_points[...], TN))
            row = i * BLOCK + lax.broadcasted_iota(jnp.int32, (BLOCK, width), 0)
            matrix[span_of(i), :] = part + jnp.where(row == lax.broadcasted_iota(jnp.int32, (BLOCK, width), 1), noise, 0.0)
            return carry

        def wave(level, carry):
            angle = dot_one(wave_ref[level].astype(bf16), basis_points[...], TN)
            matrix[pl.ds(pl.multiple_of(width + level * rank, rank), rank), :] = math.sqrt(2.0 / rank) * cosine(angle)
            return carry

        def step(k, carry):
            here = span_of(k)
            inverses[0] = inverse(matrix[here, here], jnp.min(noise), residual, approx)

            def weigh_leaf(r, carry):
                lower_ref[span_of(r - 1), here] = dot_full(matrix[span_of(r), here], inverses[0])
                return carry

            def weigh_side(r, carry):
                aug_ref[span_of(r, chunk), here] = dot_full(matrix[span_of(r, chunk, width), here], inverses[0])
                return carry

            def column(j, carry):
                there = span_of(j)

                def update_leaf(r, carry):
                    matrix[span_of(r), there] -= dot_full(lower_ref[span_of(r - 1), here], matrix[there, here], NT)
                    return carry

                def update_side(r, carry):
                    at = span_of(r, chunk, width)
                    matrix[at, there] -= dot_full(aug_ref[span_of(r, chunk), here], matrix[there, here], NT)
                    return carry

                lax.fori_loop(j, blocks, update_leaf, 0)
                return lax.fori_loop(0, side // chunk, update_side, carry)

            lax.fori_loop(k + 1, blocks, weigh_leaf, 0)
            lax.fori_loop(0, side // chunk, weigh_side, 0)
            return lax.fori_loop(k + 1, blocks, column, carry)

        lax.fori_loop(0, blocks, rebuild, 0)
        lax.fori_loop(0, levels, wave, 0)
        right_sides()
        lax.fori_loop(0, blocks, step, 0)
        for level in range(levels):
            at = sum(side - before * rank for before in range(1, level))
            kept = rest_ref if level else first_ref

            def add_rows(r, carry):
                kept[span_of(r, 8, at), :] = dot_full(
                    aug_ref[span_of(r, 8, level * rank), :], matrix[width + level * rank:width + (level + 1) * rank, :], NT)
                return carry

            lax.fori_loop(0, (side - level * rank) // 8, add_rows, 0)

    total = jnp.zeros((), f32)
    for k in range(blocks):
        build(k, k)
        total = total + jnp.max(jnp.sum(matrix[spans[k], spans[k]], axis=0, keepdims=True))
    tame = total <= TAME * jnp.min(noise)

    all_steps(dot_three)

    @pl.when(jnp.logical_not(tame))
    def _():
        all_full()


def eliminate(own, other, rank, residual, approx):
    total = own + other
    capacitance = total[:rank] + jnp.where(unit(rank), 1.0, 0.0)
    return total, dot_full(total[rank:], inverse(capacitance, jnp.float32(1.0), residual, approx))


def height_kernel(own_ref, other_ref, coefficient_ref, total_ref, residual, approx):
    total, coefficients = eliminate(own_ref[...], other_ref[...], own_ref.shape[1], residual, approx)
    coefficient_ref[...] = coefficients
    total_ref[...] = total[own_ref.shape[1]:]


def reduce_kernel(left, coefficient_ref, total_ref, own_ref, other_ref, *out_refs):
    rank = own_ref.shape[1]
    at = to = 0
    for level in range(1, left):
        start = (level - 1) * rank
        size = coefficient_ref.shape[0] - start
        value = own_ref[at:at + size, :] + other_ref[at:at + size, :] - dot_full(
            coefficient_ref[start:, :], total_ref[start:start + rank, :], NT)
        if level == 1:
            out_refs[0][...] = value
        else:
            out_refs[1][to:to + size, :] = value
            to += size
        at += size


def back_kernel(lower_ref, aug_ref, solved_ref):
    width = aug_ref.shape[1]
    spans = [slice(k * BLOCK, (k + 1) * BLOCK) for k in range(width // BLOCK)]
    for k in range(len(spans) - 1, -1, -1):
        value = aug_ref[:, spans[k]]
        for j in range(k + 1, len(spans)):
            value = value - dot_full(solved_ref[:, spans[j]], lower_ref[(j - 1) * BLOCK:j * BLOCK, spans[k]])
        solved_ref[:, spans[k]] = value


def apply_kernel(coefficient_ref, solved_ref, rest_ref):
    rank = coefficient_ref.shape[1]
    rest_ref[...] = solved_ref[rank:, :] - dot_full(coefficient_ref[...], solved_ref[:rank, :])


def final_kernel(own_ref, other_ref, solved_ref, sign_ref, target_ref, solve_ref, terms_ref, all_ref, residual, approx):
    rank = own_ref.shape[1]
    probes = sign_ref.shape[0]
    _, last = eliminate(own_ref[...], other_ref[...], rank, residual, approx)
    solved = solved_ref[rank:, :] - dot_full(last, solved_ref[:rank, :])
    solve_ref[...] = solved[:probes]
    target = solved[probes:probes + 1]
    target_ref[...] = target
    terms = (-0.5 / PROBES) * jnp.sum(sign_ref[...] * solved[:probes], axis=0, keepdims=True)
    terms_ref[...] = terms
    all_ref[...] = 0.5 * target * target + terms


def whole(count=1):
    return [pl.BlockSpec(memory_space=pltpu.VMEM)] * count


def scalars():
    return pl.BlockSpec(memory_space=pltpu.SMEM)


def shards(covariates, targets, noise_var, lengths, frequencies, phases, tree_order, probe_seeds):
    leaf_count = lax.axis_size("leaf")
    leaf_index = lax.axis_index("leaf")
    width = tree_order.shape[0]
    rank = phases.shape[1]
    probes = probe_seeds.shape[0]
    levels = leaf_count.bit_length() - 1
    tail = -(-(probes + 1) // 8) * 8
    lanes = 128
    chunks = width // lanes
    covs = covariates.shape[0]
    piece = jnp.concatenate(
        [
            covariates.reshape(covs, chunks, lanes).transpose(1, 0, 2).reshape(chunks * covs, lanes),
            targets.reshape(chunks, lanes),
            noise_var.reshape(chunks, lanes),
        ],
        axis=0,
    )
    piece = lax.optimization_barrier(piece)
    pieces = [piece]
    for k in range(2, leaf_count, 2):
        pieces.append(lax.ppermute(piece, "leaf", [(i, i ^ k) for i in range(leaf_count)]))
    near = jnp.concatenate(pieces, axis=0)
    place = leaf_index[None].astype(jnp.int32)
    sizes = [(levels - level) * rank + tail for level in range(levels)]
    params = pltpu.CompilerParams(vmem_limit_bytes=VMEM_BYTES)
    nodes = phases.shape[0]
    integers = jnp.concatenate([tree_order.reshape(chunks, lanes), jnp.pad(probe_seeds, (0, lanes - probes))[None]], axis=0)
    reals = jnp.concatenate([frequencies.reshape(nodes * covs, rank), phases, jnp.pad(lengths, (0, rank - covs))[None]], axis=0)
    code, lane, scale, waves, signs = pl.pallas_call(
        functools.partial(early_kernel, levels, nodes),
        out_shape=(
            jax.ShapeDtypeStruct((chunks, lanes), jnp.int32),
            jax.ShapeDtypeStruct((chunks, lanes), jnp.int32),
            jax.ShapeDtypeStruct((covs, lanes), f32),
            jax.ShapeDtypeStruct((levels, 8 * covs, rank), f32),
            jax.ShapeDtypeStruct((probes, width), f32),
        ),
        in_specs=[scalars()] + whole(2),
        out_specs=tuple(whole(5)),
        compiler_params=params,
        name="early",
    )(place, integers, reals)
    near, code, lane, scale, waves, signs = lax.optimization_barrier((near, code, lane, scale, waves, signs))
    far = partner_of(near, "leaf", 0)
    points = pl.pallas_call(
        near_kernel,
        out_shape=jax.ShapeDtypeStruct((3 * chunks * covs, lanes), f32),
        in_specs=whole(3),
        out_specs=whole()[0],
        compiler_params=params,
        cost_estimate=pl.CostEstimate(flops=10**9, bytes_accessed=0, transcendentals=0),
        name="near",
    )(code, lane, near)
    far, points = lax.optimization_barrier((far, points))
    side = levels * rank + tail
    lower, aug, first, later = pl.pallas_call(
        functools.partial(leaf_kernel, levels),
        out_shape=(
            jax.ShapeDtypeStruct((width - BLOCK, width - BLOCK), f32),
            jax.ShapeDtypeStruct((side, width), f32),
            jax.ShapeDtypeStruct((sizes[0], rank), f32),
            jax.ShapeDtypeStruct((sum(sizes[1:]), rank), f32),
        ),
        in_specs=whole(7),
        out_specs=tuple(whole(4)),
        scratch_shapes=[
            pltpu.VMEM((width + side, width), f32),
            pltpu.VMEM((2, BLOCK, BLOCK), f32),
            pltpu.VMEM((BLOCK, BLOCK), f32),
            pltpu.VMEM((BLOCK, BLOCK), f32),
            pltpu.VMEM((8 * covs, width), bf16),
            pltpu.VMEM((8 * covs, width), bf16),
            pltpu.VMEM((8 * covs, width), bf16),
        ],
        compiler_params=params,
        name="leaf",
    )(code, lane, scale, waves, signs, points, far)
    small = [pltpu.VMEM((rank, rank), f32), pltpu.VMEM((rank, rank), f32)]
    solved = pl.pallas_call(
        back_kernel,
        out_shape=jax.ShapeDtypeStruct((side, width), f32),
        in_specs=whole(2),
        out_specs=whole()[0],
        compiler_params=params,
        cost_estimate=pl.CostEstimate(flops=12 * side * width * width // 2, bytes_accessed=0, transcendentals=0),
        name="back",
    )(lower, aug)
    for height in range(1, levels):
        left = levels - height + 1
        other_first = partner_of(first, "leaf", height - 1)
        other_later = partner_of(later, "leaf", height - 1)
        other_first, solved = lax.optimization_barrier((other_first, solved))
        rest = side - height * rank
        coefficient, total = pl.pallas_call(
            height_kernel,
            out_shape=(jax.ShapeDtypeStruct((rest, rank), f32), jax.ShapeDtypeStruct((rest, rank), f32)),
            in_specs=whole(2),
            out_specs=tuple(whole(2)),
            scratch_shapes=small,
            compiler_params=params,
            name=f"height_{height}",
        )(first, other_first)
        outs = [jax.ShapeDtypeStruct((sizes[height], rank), f32)]
        if left > 2:
            outs.append(jax.ShapeDtypeStruct((sum(sizes[height + 1:]), rank), f32))
        found = pl.pallas_call(
            functools.partial(reduce_kernel, left),
            out_shape=tuple(outs),
            in_specs=whole(4),
            out_specs=tuple(whole(len(outs))),
            compiler_params=params,
            name=f"reduce_{height}",
        )(coefficient, total, later, other_later)
        first, later = found[0], found[-1]
        solved = pl.pallas_call(
            apply_kernel,
            out_shape=jax.ShapeDtypeStruct((rest, width), f32),
            in_specs=whole(2),
            out_specs=whole()[0],
            compiler_params=params,
            cost_estimate=pl.CostEstimate(flops=12 * rest * rank * width, bytes_accessed=0, transcendentals=0),
            name=f"apply_{height}",
        )(coefficient, solved)
    other = partner_of(first, "leaf", levels - 1)
    target_solve, probe_solves, terms, noise_grad = pl.pallas_call(
        final_kernel,
        out_shape=(
            jax.ShapeDtypeStruct((1, width), f32),
            jax.ShapeDtypeStruct((probes, width), f32),
            jax.ShapeDtypeStruct((1, width), f32),
            jax.ShapeDtypeStruct((1, width), f32),
        ),
        in_specs=whole(4),
        out_specs=tuple(whole(4)),
        scratch_shapes=small,
        compiler_params=params,
        name="final",
    )(first, other, solved, signs)
    probe_count = lax.axis_size("probe")
    for k in range(1, probe_count):
        noise_grad = noise_grad + lax.ppermute(terms, "probe", [(i, i ^ k) for i in range(probe_count)])
    return (target_solve[0], probe_solves, noise_grad[0])


def solution(mesh):
    in_specs = (P(None, "leaf"), P("leaf"), P("leaf"), P(), P(), P(), P("leaf"), P("probe"))
    out_specs = (P("leaf"), P("probe", "leaf"), P("leaf"))
    return jax.shard_map(shards, mesh=mesh, in_specs=in_specs, out_specs=out_specs, check_vma=False)
```
